256 devices in a mesh: rows: 64 (over z, y, core), grp: 4 (over x).
Axes of the slice: x: 4, y: 4, z: 8, core: 2. Of those that a mesh axis runs over, the one named last changes fastest.
Arguments:
- tiles: bfloat16 [64, 4, 48, 128, 128], P('rows', 'grp'), may hold values from -0.15625 to 0.15625
- tile_row: int32 [64, 4, 48], P('rows', 'grp'), may hold values from 0 to 7
- tile_slot: int32 [64, 4, 48], P('rows', 'grp'), may hold values from 0 to 63
- tile_count: int32 [64, 4], P('rows', 'grp'), may hold values from 6 to 48, as said below
- want: int32 [64, 64], P('rows'), may hold values from 0 to 7
- omega: bfloat16 [65536, 256], P(('rows', 'grp')), may hold values from -6 to 6
Outputs:
- basis: float32 [65536, 256], P(('rows', 'grp'))
- factor: float32 [256, 256], replicated
The draws below stay inside these ranges and needn't reach their ends.
Inputs may be any that keep to these rules, and one draw needn't show every extreme that they name: `tile_count`: some device has exactly 48 live slots in every draw; every device has 6, 12, 24 or 48.
All inputs are finite; a program needn't handle non-finite values.
Results may differ from the reference program's by a relative error of at most 0.0028.
Values may be sent and summed in bfloat16 or wider, within the bound.
A program may use at most 64 MiB of HBM per device.

```python
import math
import jax
import jax.numpy as jnp
from jax import lax

TILE = 128
K = 256
RBD = 8
TD = 48
RB = 512
NN = 65536
N_ROWS = 64
N_GRP = 4


def draw_tile_count(key, part):
    key = jax.random.fold_in(key, 11)
    first_key, second_key = jax.random.split(key)
    shifts = jax.random.randint(first_key, (N_ROWS, N_GRP), 0, 4)
    chosen = jax.random.randint(second_key, (), 0, N_ROWS * N_GRP)
    places = jnp.arange(N_ROWS * N_GRP).reshape(N_ROWS, N_GRP)
    shifts = jnp.where(places == chosen, 0, shifts)
    return jnp.right_shift(jnp.full((N_ROWS, N_GRP), TD, jnp.int32), shifts.astype(jnp.int32)).astype(jnp.int32)


def set_ends(values, rng, least, largest):
    dims = values.shape
    spot = [jax.random.randint(jax.random.fold_in(rng, axis), (), 0, dims[axis]) for axis in range(len(dims))]
    values = values.at[tuple(spot)].set(least)
    longest = dims.index(max(dims))
    spot[longest] = (spot[longest] + 1) % dims[longest]
    return values.at[tuple(spot)].set(largest)


def block_scale(stream_key, shape, pieces, low, largest):
    def one(position, shards_of):
        steps = jax.random.uniform(jax.random.fold_in(jax.random.fold_in(stream_key, 6), position), (shards_of,), jnp.float32, low / len(pieces), largest / len(pieces))
        return jnp.repeat(jnp.exp(steps), shape[position] // shards_of).reshape((-1,) + (1,) * (len(shape) - position - 1))

    gain = one(*pieces[0])
    for cut in pieces[1:]:
        gain = gain * one(*cut)
    return gain


def centred(key, extent, scale, bound, shards=(), held_as=jnp.bfloat16):
    gain = block_scale(key, extent, shards, -0.22, 0.18) if shards else 1.0
    entries = jax.random.normal(key, extent, jnp.float32) * scale * gain
    return jnp.minimum(jnp.maximum(entries, -bound), bound).astype(held_as)


def setup_inputs(seed: int = 0) -> dict:
    seeds = jax.random.split(jax.random.key(seed), 7)
    tiles = centred(seeds[0], (N_ROWS, N_GRP, TD, TILE, TILE), (TILE * TD * N_GRP // (2 * RBD)) ** -0.5, 0.15625, ((0, 64), (1, 4)))
    tile_row = set_ends(jax.random.randint(seeds[1], (N_ROWS, N_GRP, TD), 0, RBD), jax.random.fold_in(seeds[1], 1), 0, RBD - 1).astype(jnp.int32)
    tile_slot = set_ends(jax.random.randint(seeds[2], (N_ROWS, N_GRP, TD), 0, N_ROWS), jax.random.fold_in(seeds[2], 1), 0, N_ROWS - 1).astype(jnp.int32)
    tile_count = draw_tile_count(jax.random.fold_in(seeds[6], 71), 0)
    want = set_ends(jax.random.randint(seeds[4], (N_ROWS, N_ROWS), 0, RBD), jax.random.fold_in(seeds[4], 1), 0, RBD - 1).astype(jnp.int32)
    omega = centred(seeds[5], (NN, K), 1.0, 6.0, ((0, 256),))
    return {"tiles": tiles, "tile_row": tile_row, "tile_slot": tile_slot, "tile_count": tile_count, "want": want, "omega": omega}


def apply_tiles(source, block_tiles, row_ids, col_ids, live_mask, transpose):

    def add_device(running, device_data):
        dev_tiles, dev_rows, dev_cols, dev_live = device_data
        weights = dev_live.astype(jnp.float32)[:, None, None]
        if transpose:
            inputs = source[dev_rows].astype(jnp.float32)
            product = jnp.einsum('tba,tbk->tak', dev_tiles.astype(jnp.float32), inputs)
            return (running.at[dev_cols].add(product * weights), None)
        inputs = source[dev_cols].astype(jnp.float32)
        product = jnp.einsum('tab,tbk->tak', dev_tiles.astype(jnp.float32), inputs)
        return (running.at[dev_rows].add(product * weights), None)
    start = jnp.zeros((RB, TILE, K), jnp.float32)
    return lax.scan(add_device, start, (block_tiles, row_ids, col_ids, live_mask))[0]

def reference(tiles, tile_row, tile_slot, tile_count, want, omega):
    devices = N_ROWS * N_GRP
    block_tiles = tiles.reshape(devices, TD, TILE, TILE)
    row_ids = (jnp.arange(N_ROWS, dtype=jnp.int32)[:, None, None] * RBD + tile_row).reshape(devices, TD).astype(jnp.int32)
    slot_ids = tile_slot.reshape(devices, TD).astype(jnp.int32)
    wanted = jnp.repeat(want, N_GRP, axis=0).astype(jnp.int32)
    col_ids = (slot_ids * RBD + jnp.take_along_axis(wanted, slot_ids, axis=1)).astype(jnp.int32)
    live_mask = jnp.arange(TD, dtype=jnp.int32)[None, :] < tile_count.reshape(devices, 1)
    omega_blocks = omega.reshape(RB, TILE, K)
    z_full = apply_tiles(omega_blocks, block_tiles, row_ids, col_ids, live_mask, False).astype(jnp.bfloat16)
    w_full = apply_tiles(z_full, block_tiles, row_ids, col_ids, live_mask, True).astype(jnp.bfloat16)
    y_full = apply_tiles(w_full, block_tiles, row_ids, col_ids, live_mask, False).reshape(NN, K)
    gram_sum = jnp.dot(y_full.T.astype(jnp.float32), y_full.astype(jnp.float32), precision=lax.Precision.HIGHEST, preferred_element_type=jnp.float32)
    factor_low = jnp.linalg.cholesky(gram_sum)
    norm_scale = math.sqrt(NN)
    basis_out = lax.linalg.triangular_solve(factor_low, y_full, left_side=False, lower=True, transpose_a=True) * norm_scale
    return (basis_out, factor_low.T / norm_scale)
```

```python
import functools
import math

import jax
import jax.numpy as jnp
from jax import lax
from jax.experimental import pallas as pl
from jax.experimental.pallas import tpu as pltpu
from jax.sharding import PartitionSpec as P

RBD = 8
LANES = 128
MESH = pl.DeviceIdType.MESH
SLOT, ROW, PREV_ROW, PREV_SLOT, LAST_ROW, LAST_SLOT = range(6)


def chains(tile_row, tile_slot, tile_count):
    total = tile_row.shape[0]
    order = jnp.arange(total, dtype=jnp.int32)
    live = order < tile_count
    lane = jnp.arange(LANES, dtype=jnp.int32)
    pad = lambda values: jnp.pad(values, (0, LANES - total))
    keys = jnp.stack([tile_row, tile_slot, tile_row, tile_slot])
    query = jnp.stack([pad(tile_row), pad(tile_slot), lane, lane])
    bound = jnp.stack([lane, lane, jnp.full_like(lane, total), jnp.full_like(lane, total)])
    hit = (keys[:, None, :] == query[:, :, None]) & live & (order < bound[:, :, None])
    found = jnp.max(jnp.where(hit, order + 1, 0), axis=2)
    head = jnp.stack([pad(tile_slot), pad(tile_row)])
    return jnp.concatenate([head, found, jnp.zeros((2, LANES), jnp.int32)], axis=0)


def apply_kernel(
    n_rows, n_grp, slots, chunks,
    tiles_ref, omega_ref, meta_ref, want_ref, out_ref,
    tbuf, meta_all, meta_s, want_all, want_s, prev_v, prev_s, last_v, last_s,
    omega_all, ghosts, ghost_out, partial, z_blocks,
    contrib_out, contrib_in, w_partial, w_blocks, w_ghosts, w_ghost_out, y_blocks, y_in,
    local_sem, small_send, small_recv, omega_send, omega_recv, want_send, want_recv,
    right_send, right_recv, left_send, left_recv, fwd_send, fwd_recv,
    ghost_send, ghost_recv, contrib_send, contrib_recv, wg_send, wg_recv, y_send, y_recv,
):
    me = lax.axis_index("rows")
    grp = lax.axis_index("grp")
    per = slots // chunks
    owned = RBD // n_grp
    group = lambda step: lax.rem(grp + step, n_grp)
    peer = lambda step: lax.rem(me + step, n_rows)
    right, left = group(1), group(n_grp - 1)

    barrier = pltpu.get_barrier_semaphore()

    def greet(step, carry):
        pl.semaphore_signal(barrier, inc=1, device_id={"rows": peer(step)}, device_id_type=MESH)
        return carry

    for step in range(1, n_grp):
        pl.semaphore_signal(barrier, inc=1, device_id={"grp": group(step)}, device_id_type=MESH)
    lax.fori_loop(1, n_rows, greet, 0)
    pl.semaphore_wait(barrier, n_rows - 1 + n_grp - 1)

    def over_x(src, dst, send, recv, to):
        return pltpu.make_async_remote_copy(
            src_ref=src, dst_ref=dst, send_sem=send, recv_sem=recv, device_id={"grp": to}, device_id_type=MESH)

    def over_rows(src, dst, send, recv, to):
        return pltpu.make_async_remote_copy(
            src_ref=src, dst_ref=dst, send_sem=send, recv_sem=recv, device_id={"rows": to}, device_id_type=MESH)

    def want_copy(step):
        return over_rows(want_ref, want_all.at[me], want_send.at[step], want_recv.at[step], peer(step))

    def want_arrival(step):
        came = lax.rem(me - step + n_rows, n_rows)
        return over_rows(want_ref, want_all.at[came], want_send.at[step], want_recv.at[step], peer(step))

    def meta_copy(step):
        place = (0, 1, 3, 2)[step]
        return over_x(meta_ref, meta_all.at[place], small_send.at[step], small_recv.at[step], group(step))

    def omega_copy(step):
        to = group(step)
        return over_x(
            omega_ref.at[to], omega_all.at[pl.ds(grp * owned, owned)], omega_send.at[step], omega_recv.at[step], to)

    def omega_arrival(step):
        came = group(n_grp - step)
        return over_x(
            omega_ref.at[came], omega_all.at[pl.ds(came * owned, owned)], omega_send.at[step], omega_recv.at[step], came)

    def start_want(step, carry):
        want_copy(step).start()
        return carry

    lax.fori_loop(1, n_rows, start_want, 0)
    for step in range(1, n_grp):
        omega_copy(step).start()
        meta_copy(step).start()

    own_tiles = pltpu.make_async_copy(tiles_ref, tbuf.at[0], local_sem.at[0])
    own_tiles.start()

    def to_right(c):
        part = pl.ds(c * per, per)
        return over_x(tiles_ref.at[part], tbuf.at[1, part], right_send.at[c], right_recv.at[c], right)

    def to_left(c):
        part = pl.ds(c * per, per)
        return over_x(tiles_ref.at[part], tbuf.at[2, part], left_send.at[c], left_recv.at[c], left)

    def forward(c):
        part = pl.ds(c * per, per)
        if c < chunks // 2:
            return over_x(tbuf.at[1, part], tbuf.at[3, part], fwd_send.at[c], fwd_recv.at[c], right)
        return over_x(tbuf.at[2, part], tbuf.at[3, part], fwd_send.at[c], fwd_recv.at[c], left)

    for c in range(chunks):
        to_right(c).start()
        to_left(c).start()

    want_all[me] = want_ref[...]
    for j in range(owned):
        omega_all[grp * owned + j] = omega_ref[grp, j]
    meta_all[0] = meta_ref[...]
    partial[:, 0] = jnp.zeros((n_grp,) + partial.shape[2:], jnp.float32)
    w_partial[0] = jnp.zeros(w_partial.shape[1:], jnp.float32)

    def wait_want(step, carry):
        want_arrival(step).wait_recv()
        return carry

    lax.fori_loop(1, n_rows, wait_want, 0)
    want_down = pltpu.make_async_copy(want_all, want_s, local_sem.at[1])
    want_down.start()
    for step in range(1, n_grp):
        meta_copy(step).wait_recv()
        omega_arrival(step).wait_recv()
    meta_down = pltpu.make_async_copy(meta_all, meta_s, local_sem.at[2])
    meta_down.start()
    want_down.wait()
    meta_down.wait()

    def ghost_copy(step):
        return over_rows(ghost_out.at[step], ghosts.at[step], ghost_send.at[step], ghost_recv.at[step], peer(step))

    def start_ghost(step, carry):
        ghost_out[step] = omega_all[want_s[peer(step), 0, me]]
        ghost_copy(step).start()
        return carry

    ghosts[0] = omega_all[want_s[me, 0, me]]
    lax.fori_loop(1, n_rows, start_ghost, 0)

    blocks = lax.broadcasted_iota(jnp.int32, (RBD, LANES), 0)

    def link(step, last):
        row = want_all[lax.rem(me - step + n_rows, n_rows)]
        hit = blocks == row
        prev_v[step] = jnp.max(jnp.where(hit, last, 0), axis=0, keepdims=True)
        return jnp.where(hit, step + 1, last)

    last_v[...] = lax.fori_loop(0, n_rows, link, jnp.zeros((RBD, LANES), jnp.int32))
    prev_down = pltpu.make_async_copy(prev_v, prev_s, local_sem.at[1])
    last_down = pltpu.make_async_copy(last_v, last_s, local_sem.at[2])
    prev_down.start()
    last_down.start()
    prev_down.wait()
    last_down.wait()

    own_tiles.wait()
    for c in range(chunks):
        to_right(c).wait_recv()
        if c < chunks // 2:
            forward(c).start()
        to_left(c).wait_recv()
        if c >= chunks // 2:
            forward(c).start()

    def wait_ghost(step, carry):
        ghost_copy(step).wait_recv()
        return carry

    lax.fori_loop(1, n_rows, wait_ghost, 0)

    unroll = per

    def multiply(place, first, source, by_row, sent):
        prev_key = PREV_ROW if by_row else PREV_SLOT
        products = []
        for i in range(unroll):
            t = first + i
            tile = tbuf[place, t]
            if by_row:
                slot = meta_s[place, SLOT, t]
                block = source[lax.rem(me - slot + n_rows, n_rows)]
                product = lax.dot_general(block, tile, (((1,), (1,)), ((), ())), preferred_element_type=jnp.float32)
            else:
                block = source[meta_s[place, ROW, t]]
                product = lax.dot_general(block, tile, (((1,), (0,)), ((), ())), preferred_element_type=jnp.float32)
            products.append(product)
        for i in range(unroll):
            t = first + i
            partial[place, t + 1] = products[i] + partial[place, meta_s[place, prev_key, t]]

    def whole(place, source, by_row):
        def step(c, carry):
            multiply(place, c * unroll, source, by_row, None)
            return carry
        lax.fori_loop(0, slots // unroll, step, 0)

    def total(key, index):
        value = partial[0, meta_s[0, key, index]]
        for place in range(1, n_grp):
            value = value + partial[place, meta_s[place, key, index]]
        return value

    for place in range(3):
        whole(place, ghosts, True)
    for c in range(chunks):
        forward(c).wait_recv()
        multiply(3, c * per, ghosts, True, None)

    def close_z(b, carry):
        z_blocks[b] = total(LAST_ROW, b).astype(jnp.bfloat16)
        return carry

    lax.fori_loop(0, RBD, close_z, 0)

    for place in range(n_grp):
        whole(place, z_blocks, False)

    def contrib_copy(step):
        return over_rows(
            contrib_out.at[step], contrib_in.at[step], contrib_send.at[step], contrib_recv.at[step], peer(step))

    contrib_in[0] = total(LAST_SLOT, me).astype(jnp.bfloat16)

    def start_contrib(step, carry):
        contrib_out[step] = total(LAST_SLOT, peer(step)).astype(jnp.bfloat16)
        contrib_copy(step).start()
        return carry

    lax.fori_loop(1, n_rows, start_contrib, 0)

    def add_contrib(step):
        w_partial[step + 1] = contrib_in[step].astype(jnp.float32) + w_partial[prev_s[step, 0, me]]

    add_contrib(0)

    def take_contrib(step, carry):
        contrib_copy(step).wait_recv()
        add_contrib(step)
        return carry

    lax.fori_loop(1, n_rows, take_contrib, 0)

    def close_w(b, carry):
        w_blocks[b] = w_partial[last_s[b, me]].astype(jnp.bfloat16)
        return carry

    lax.fori_loop(0, RBD, close_w, 0)

    def wg_copy(step):
        return over_rows(w_ghost_out.at[step], w_ghosts.at[step], wg_send.at[step], wg_recv.at[step], peer(step))

    def start_wg(step, carry):
        w_ghost_out[step] = w_blocks[want_s[peer(step), 0, me]]
        wg_copy(step).start()
        return carry

    def wait_wg(step, carry):
        wg_copy(step).wait_recv()
        return carry

    w_ghosts[0] = w_blocks[want_s[me, 0, me]]
    lax.fori_loop(1, n_rows, start_wg, 0)
    lax.fori_loop(1, n_rows, wait_wg, 0)

    for place in range(n_grp):
        whole(place, w_ghosts, True)

    def close_y(b, carry):
        y_blocks[b] = total(LAST_ROW, b)
        return carry

    lax.fori_loop(0, RBD, close_y, 0)

    def y_copy(step):
        to = group(step)
        return over_x(
            y_blocks.at[pl.ds(to * owned, owned)], y_in.at[step], y_send.at[step], y_recv.at[step], to)

    for step in range(1, n_grp):
        y_copy(step).start()
    for j in range(owned):
        y_in[0, j] = y_blocks[grp * owned + j]
    for step in range(1, n_grp):
        y_copy(step).wait_recv()
    width = out_ref.shape[0] // n_grp
    for step in range(n_grp):
        came = group(n_grp - step) if step else grp
        for j in range(owned):
            out_ref[pl.ds(pl.multiple_of(came * width, width), width), pl.ds(j * LANES, LANES)] = y_in[step, j]

    def drain(step, carry):
        want_copy(step).wait_send()
        ghost_copy(step).wait_send()
        contrib_copy(step).wait_send()
        wg_copy(step).wait_send()
        return carry

    lax.fori_loop(1, n_rows, drain, 0)
    for step in range(1, n_grp):
        meta_copy(step).wait_send()
        omega_copy(step).wait_send()
        y_copy(step).wait_send()
    for c in range(chunks):
        to_right(c).wait_send()
        to_left(c).wait_send()
        forward(c).wait_send()


def apply_all(tiles, omega_parts, meta, want_row, n_rows, n_grp, chunks):
    slots, tile, _ = tiles.shape
    owned = RBD // n_grp
    width = omega_parts.shape[2]
    block = (width, tile)
    bf16, f32, i32 = jnp.bfloat16, jnp.float32, jnp.int32
    dma = lambda count: pltpu.SemaphoreType.DMA((count,))
    vmem = pl.BlockSpec(memory_space=pltpu.VMEM)
    scratch = [
        pltpu.VMEM((n_grp, slots, tile, tile), bf16),
        pltpu.VMEM((n_grp, 8, LANES), i32),
        pltpu.SMEM((n_grp, 8, LANES), i32),
        pltpu.VMEM((n_rows, 1, LANES), i32),
        pltpu.SMEM((n_rows, 1, LANES), i32),
        pltpu.VMEM((n_rows, 1, LANES), i32),
        pltpu.SMEM((n_rows, 1, LANES), i32),
        pltpu.VMEM((RBD, LANES), i32),
        pltpu.SMEM((RBD, LANES), i32),
        pltpu.VMEM((RBD,) + block, bf16),
        pltpu.VMEM((n_rows,) + block, bf16),
        pltpu.VMEM((n_rows,) + block, bf16),
        pltpu.VMEM((n_grp, slots + 1) + block, f32),
        pltpu.VMEM((RBD,) + block, bf16),
        pltpu.VMEM((n_rows,) + block, bf16),
        pltpu.VMEM((n_rows,) + block, bf16),
        pltpu.VMEM((n_rows + 1,) + block, f32),
        pltpu.VMEM((RBD,) + block, bf16),
        pltpu.VMEM((n_rows,) + block, bf16),
        pltpu.VMEM((n_rows,) + block, bf16),
        pltpu.VMEM((RBD,) + block, f32),
        pltpu.VMEM((n_grp, owned) + block, f32),
        dma(3), dma(n_grp), dma(n_grp), dma(n_grp), dma(n_grp), dma(n_rows), dma(n_rows),
        dma(chunks), dma(chunks), dma(chunks), dma(chunks), dma(chunks), dma(chunks),
        dma(n_rows), dma(n_rows), dma(n_rows), dma(n_rows), dma(n_rows), dma(n_rows), dma(n_grp), dma(n_grp),
    ]
    return pl.pallas_call(
        functools.partial(apply_kernel, n_rows, n_grp, slots, chunks),
        out_shape=jax.ShapeDtypeStruct((width * n_grp, owned * tile), f32),
        in_specs=[pl.BlockSpec(memory_space=pl.ANY), vmem, vmem, vmem],
        out_specs=vmem,
        scratch_shapes=scratch,
        compiler_params=pltpu.CompilerParams(
            collective_id=0, has_side_effects=True, vmem_limit_bytes=40 * 1024 * 1024),
        name="apply_all",
    )(tiles, omega_parts, meta, want_row)


def per_device(tiles, tile_row, tile_slot, tile_count, want, omega):
    tile = tiles.shape[-1]
    slots = tiles.shape[2]
    columns = omega.shape[1]
    n_rows = lax.axis_size("rows")
    n_grp = lax.axis_size("grp")
    highest = lax.Precision.HIGHEST
    chunks = 8 if slots % 8 == 0 and slots >= 48 else 2
    owned = RBD // n_grp
    meta = chains(tile_row.reshape(slots), tile_slot.reshape(slots), tile_count.reshape(()))
    want_row = jnp.pad(want.reshape(1, n_rows), ((0, 0), (0, LANES - n_rows)))
    omega_parts = omega.reshape(owned, tile, n_grp, columns // n_grp).transpose(2, 0, 3, 1)
    y_t = apply_all(tiles.reshape(slots, tile, tile), omega_parts, meta, want_row, n_rows, n_grp, chunks)
    partial_gram = lax.dot_general(
        y_t, y_t, (((1,), (1,)), ((), ())), precision=highest, preferred_element_type=jnp.float32)
    gram = lax.psum(lax.psum(partial_gram, "grp"), "rows")
    factor_low = jnp.linalg.cholesky(gram)
    norm_scale = math.sqrt(n_rows * RBD * tile)
    basis = (
        lax.linalg.triangular_solve(factor_low, y_t.T, left_side=False, lower=True, transpose_a=True) * norm_scale
    )
    return (basis, factor_low.T / norm_scale)


def solution(mesh):
    return jax.shard_map(
        per_device,
        mesh=mesh,
        in_specs=(
            P("rows", "grp", None, None, None),
            P("rows", "grp", None),
            P("rows", "grp", None),
            P("rows", "grp"),
            P("rows", None),
            P(("rows", "grp"), None),
        ),
        out_specs=(P(("rows", "grp"), None), P()),
        check_vma=False,
    )
```

```python
import functools
import math

import jax
import jax.numpy as jnp
from jax import lax
from jax.experimental import pallas as pl
from jax.experimental.pallas import tpu as pltpu
from jax.sharding import PartitionSpec as P

RBD = 8
LANES = 128
MESH = pl.DeviceIdType.MESH
SLOT, ROW, PREV_ROW, PREV_SLOT, LAST_ROW, LAST_SLOT = range(6)


def chains(tile_row, tile_slot, tile_count):
    total = tile_row.shape[0]
    order = jnp.arange(total, dtype=jnp.int32)
    live = order < tile_count
    lane = jnp.arange(LANES, dtype=jnp.int32)
    pad = lambda values: jnp.pad(values, (0, LANES - total))
    keys = jnp.stack([tile_row, tile_slot, tile_row, tile_slot])
    query = jnp.stack([pad(tile_row), pad(tile_slot), lane, lane])
    bound = jnp.stack([lane, lane, jnp.full_like(lane, total), jnp.full_like(lane, total)])
    hit = (keys[:, None, :] == query[:, :, None]) & live & (order < bound[:, :, None])
    found = jnp.max(jnp.where(hit, order + 1, 0), axis=2)
    head = jnp.stack([pad(tile_slot), pad(tile_row)])
    return jnp.concatenate([head, found, jnp.zeros((2, LANES), jnp.int32)], axis=0)


def apply_kernel(
    n_rows, n_grp, slots, chunks,
    tiles_ref, omega_ref, meta_ref, want_ref, basis_ref, factor_ref,
    tbuf, meta_all, meta_s, want_all, want_s, prev_v, prev_s, last_v, last_s,
    omega_all, ghosts, ghost_out, partial, z_blocks,
    contrib_out, contrib_in, w_partial, w_blocks, w_ghosts, w_ghost_out, y_blocks, y_in,
    y_all, gram_out, gram_in, part_out, part_in, row_out, row_in, slice_all, gram_all, work,
    local_sem, small_send, small_recv, omega_send, omega_recv, want_send, want_recv,
    right_send, right_recv, left_send, left_recv, fwd_send, fwd_recv,
    ghost_send, ghost_recv, contrib_send, contrib_recv, wg_send, wg_recv, y_send, y_recv,
    gram_send, gram_recv, part_send, part_recv, row_send, row_recv, back_send, back_recv, all_send, all_recv,
):
    me = lax.axis_index("rows")
    grp = lax.axis_index("grp")
    per = slots // chunks
    owned = RBD // n_grp
    group = lambda step: lax.rem(grp + step, n_grp)
    peer = lambda step: lax.rem(me + step, n_rows)
    right, left = group(1), group(n_grp - 1)

    barrier = pltpu.get_barrier_semaphore()

    def greet(step, carry):
        pl.semaphore_signal(barrier, inc=1, device_id={"rows": peer(step)}, device_id_type=MESH)
        return carry

    for step in range(1, n_grp):
        pl.semaphore_signal(barrier, inc=1, device_id={"grp": group(step)}, device_id_type=MESH)
    lax.fori_loop(1, n_rows, greet, 0)
    pl.semaphore_wait(barrier, n_rows - 1 + n_grp - 1)

    def over_x(src, dst, send, recv, to):
        return pltpu.make_async_remote_copy(
            src_ref=src, dst_ref=dst, send_sem=send, recv_sem=recv, device_id={"grp": to}, device_id_type=MESH)

    def over_rows(src, dst, send, recv, to):
        return pltpu.make_async_remote_copy(
            src_ref=src, dst_ref=dst, send_sem=send, recv_sem=recv, device_id={"rows": to}, device_id_type=MESH)

    def want_copy(step):
        return over_rows(want_ref, want_all.at[me], want_send.at[step], want_recv.at[step], peer(step))

    def want_arrival(step):
        came = lax.rem(me - step + n_rows, n_rows)
        return over_rows(want_ref, want_all.at[came], want_send.at[step], want_recv.at[step], peer(step))

    def meta_copy(step):
        place = (0, 1, 3, 2)[step]
        return over_x(meta_ref, meta_all.at[place], small_send.at[step], small_recv.at[step], group(step))

    def omega_copy(step):
        to = group(step)
        return over_x(
            omega_ref.at[to], omega_all.at[pl.ds(grp * owned, owned)], omega_send.at[step], omega_recv.at[step], to)

    def omega_arrival(step):
        came = group(n_grp - step)
        return over_x(
            omega_ref.at[came], omega_all.at[pl.ds(came * owned, owned)], omega_send.at[step], omega_recv.at[step], came)

    def start_want(step, carry):
        want_copy(step).start()
        return carry

    lax.fori_loop(1, n_rows, start_want, 0)
    for step in range(1, n_grp):
        omega_copy(step).start()
        meta_copy(step).start()

    own_tiles = pltpu.make_async_copy(tiles_ref, tbuf.at[0], local_sem.at[0])
    own_tiles.start()

    def to_right(c):
        part = pl.ds(c * per, per)
        return over_x(tiles_ref.at[part], tbuf.at[1, part], right_send.at[c], right_recv.at[c], right)

    def to_left(c):
        part = pl.ds(c * per, per)
        return over_x(tiles_ref.at[part], tbuf.at[2, part], left_send.at[c], left_recv.at[c], left)

    def forward(c):
        part = pl.ds(c * per, per)
        if c < chunks // 2:
            return over_x(tbuf.at[1, part], tbuf.at[3, part], fwd_send.at[c], fwd_recv.at[c], right)
        return over_x(tbuf.at[2, part], tbuf.at[3, part], fwd_send.at[c], fwd_recv.at[c], left)

    for c in range(chunks):
        to_right(c).start()
        to_left(c).start()

    want_all[me] = want_ref[...]
    for j in range(owned):
        omega_all[grp * owned + j] = omega_ref[grp, j]
    meta_all[0] = meta_ref[...]
    partial[:, 0] = jnp.zeros((n_grp,) + partial.shape[2:], jnp.float32)
    w_partial[0] = jnp.zeros(w_partial.shape[1:], jnp.float32)

    def wait_want(step, carry):
        want_arrival(step).wait_recv()
        return carry

    lax.fori_loop(1, n_rows, wait_want, 0)
    want_down = pltpu.make_async_copy(want_all, want_s, local_sem.at[1])
    want_down.start()
    for step in range(1, n_grp):
        meta_copy(step).wait_recv()
        omega_arrival(step).wait_recv()
    meta_down = pltpu.make_async_copy(meta_all, meta_s, local_sem.at[2])
    meta_down.start()
    want_down.wait()
    meta_down.wait()

    def ghost_copy(step):
        return over_rows(ghost_out.at[step], ghosts.at[step], ghost_send.at[step], ghost_recv.at[step], peer(step))

    def start_ghost(step, carry):
        ghost_out[step] = omega_all[want_s[peer(step), 0, me]]
        ghost_copy(step).start()
        return carry

    ghosts[0] = omega_all[want_s[me, 0, me]]
    lax.fori_loop(1, n_rows, start_ghost, 0)

    blocks = lax.broadcasted_iota(jnp.int32, (RBD, LANES), 0)

    def link(step, last):
        row = want_all[lax.rem(me - step + n_rows, n_rows)]
        hit = blocks == row
        prev_v[step] = jnp.max(jnp.where(hit, last, 0), axis=0, keepdims=True)
        return jnp.where(hit, step + 1, last)

    last_v[...] = lax.fori_loop(0, n_rows, link, jnp.zeros((RBD, LANES), jnp.int32))
    prev_down = pltpu.make_async_copy(prev_v, prev_s, local_sem.at[1])
    last_down = pltpu.make_async_copy(last_v, last_s, local_sem.at[2])
    prev_down.start()
    last_down.start()
    prev_down.wait()
    last_down.wait()

    own_tiles.wait()
    for c in range(chunks):
        to_right(c).wait_recv()
        if c < chunks // 2:
            forward(c).start()
        to_left(c).wait_recv()
        if c >= chunks // 2:
            forward(c).start()

    def wait_ghost(step, carry):
        ghost_copy(step).wait_recv()
        return carry

    lax.fori_loop(1, n_rows, wait_ghost, 0)

    unroll = per

    def multiply(place, first, source, by_row, sent):
        prev_key = PREV_ROW if by_row else PREV_SLOT
        products = []
        for i in range(unroll):
            t = first + i
            tile = tbuf[place, t]
            if by_row:
                slot = meta_s[place, SLOT, t]
                block = source[lax.rem(me - slot + n_rows, n_rows)]
                product = lax.dot_general(block, tile, (((1,), (1,)), ((), ())), preferred_element_type=jnp.float32)
            else:
                block = source[meta_s[place, ROW, t]]
                product = lax.dot_general(block, tile, (((1,), (0,)), ((), ())), preferred_element_type=jnp.float32)
            products.append(product)
        for i in range(unroll):
            t = first + i
            partial[place, t + 1] = products[i] + partial[place, meta_s[place, prev_key, t]]

    def whole(place, source, by_row):
        def step(c, carry):
            multiply(place, c * unroll, source, by_row, None)
            return carry
        lax.fori_loop(0, slots // unroll, step, 0)

    def total(key, index):
        value = partial[0, meta_s[0, key, index]]
        for place in range(1, n_grp):
            value = value + partial[place, meta_s[place, key, index]]
        return value

    for place in range(3):
        whole(place, ghosts, True)
    for c in range(chunks):
        forward(c).wait_recv()
        multiply(3, c * per, ghosts, True, None)

    def close_z(b, carry):
        z_blocks[b] = total(LAST_ROW, b).astype(jnp.bfloat16)
        return carry

    lax.fori_loop(0, RBD, close_z, 0)

    for place in range(n_grp):
        whole(place, z_blocks, False)

    def contrib_copy(step):
        return over_rows(
            contrib_out.at[step], contrib_in.at[step], contrib_send.at[step], contrib_recv.at[step], peer(step))

    contrib_in[0] = total(LAST_SLOT, me).astype(jnp.bfloat16)

    def start_contrib(step, carry):
        contrib_out[step] = total(LAST_SLOT, peer(step)).astype(jnp.bfloat16)
        contrib_copy(step).start()
        return carry

    lax.fori_loop(1, n_rows, start_contrib, 0)

    def add_contrib(step):
        w_partial[step + 1] = contrib_in[step].astype(jnp.float32) + w_partial[prev_s[step, 0, me]]

    add_contrib(0)

    def take_contrib(step, carry):
        contrib_copy(step).wait_recv()
        add_contrib(step)
        return carry

    lax.fori_loop(1, n_rows, take_contrib, 0)

    def close_w(b, carry):
        w_blocks[b] = w_partial[last_s[b, me]].astype(jnp.bfloat16)
        return carry

    lax.fori_loop(0, RBD, close_w, 0)

    def wg_copy(step):
        return over_rows(w_ghost_out.at[step], w_ghosts.at[step], wg_send.at[step], wg_recv.at[step], peer(step))

    def start_wg(step, carry):
        w_ghost_out[step] = w_blocks[want_s[peer(step), 0, me]]
        wg_copy(step).start()
        return carry

    def wait_wg(step, carry):
        wg_copy(step).wait_recv()
        return carry

    w_ghosts[0] = w_blocks[want_s[me, 0, me]]
    lax.fori_loop(1, n_rows, start_wg, 0)
    lax.fori_loop(1, n_rows, wait_wg, 0)

    for place in range(n_grp):
        whole(place, w_ghosts, True)

    def close_y(b, carry):
        y_blocks[b] = total(LAST_ROW, b)
        return carry

    lax.fori_loop(0, RBD, close_y, 0)

    def y_copy(step):
        to = group(step)
        return over_x(
            y_blocks.at[pl.ds(to * owned, owned)], y_in.at[step], y_send.at[step], y_recv.at[step], to)

    for step in range(1, n_grp):
        y_copy(step).start()
    for j in range(owned):
        y_in[0, j] = y_blocks[grp * owned + j]
    for step in range(1, n_grp):
        y_copy(step).wait_recv()
    width = y_all.shape[0] // n_grp
    for step in range(n_grp):
        came = group(n_grp - step)
        for j in range(owned):
            y_all[pl.ds(pl.multiple_of(came * width, width), width), pl.ds(j * LANES, LANES)] = y_in[step, j]

    inner = part_in.shape[0]
    outer = n_rows // inner
    some = part_in.shape[1]
    spot = lax.rem(me, inner)
    level = lax.div(me, inner)
    y_value = y_all[...]
    own_gram = lax.dot_general(
        y_value, y_value, (((1,), (1,)), ((), ())), precision=lax.Precision.HIGHEST, preferred_element_type=jnp.float32)
    gram_out[...] = own_gram.reshape(gram_out.shape)

    def gram_copy(step):
        to = group(step)
        return over_x(gram_out.at[to], gram_in.at[grp], gram_send.at[step], gram_recv.at[step], to)

    def gram_arrival(step):
        came = group(n_grp - step)
        return over_x(gram_out.at[came], gram_in.at[came], gram_send.at[step], gram_recv.at[step], came)

    for step in range(1, n_grp):
        gram_copy(step).start()
    gram_in[grp] = gram_out[grp]
    for step in range(1, n_grp):
        gram_arrival(step).wait_recv()
    summed = gram_in[0]
    for step in range(1, n_grp):
        summed = summed + gram_in[step]
    part_out[...] = summed.reshape(part_out.shape)

    def beside(step):
        return lax.rem(spot + step, inner)

    def part_copy(step):
        to = beside(step)
        return over_rows(
            part_out.at[to], part_in.at[spot], part_send.at[step], part_recv.at[step], level * inner + to)

    def part_arrival(step):
        came = beside(inner - step)
        return over_rows(
            part_out.at[came], part_in.at[came], part_send.at[step], part_recv.at[step], level * inner + came)

    for step in range(1, inner):
        part_copy(step).start()
    part_in[spot] = part_out[spot]
    for step in range(1, inner):
        part_arrival(step).wait_recv()
    summed = part_in[0]
    for step in range(1, inner):
        summed = summed + part_in[step]
    row_out[...] = summed

    def across(step):
        return lax.rem(level + step, outer)

    def row_copy(step):
        return over_rows(
            row_out, row_in.at[level], row_send.at[step], row_recv.at[step], across(step) * inner + spot)

    def row_arrival(step):
        came = across(outer - step)
        return over_rows(row_out, row_in.at[came], row_send.at[step], row_recv.at[step], came * inner + spot)

    for step in range(1, outer):
        row_copy(step).start()
    row_in[level] = row_out[...]
    for step in range(1, outer):
        row_arrival(step).wait_recv()
    summed = row_in[0]
    for step in range(1, outer):
        summed = summed + row_in[step]
    slice_all[spot] = summed

    def back_copy(step):
        return over_rows(
            slice_all.at[spot], slice_all.at[spot], back_send.at[step], back_recv.at[step],
            level * inner + beside(step))

    def back_arrival(step):
        came = beside(inner - step)
        return over_rows(
            slice_all.at[came], slice_all.at[came], back_send.at[step], back_recv.at[step], level * inner + came)

    for step in range(1, inner):
        back_copy(step).start()
    for step in range(1, inner):
        back_arrival(step).wait_recv()
    gram_all[grp] = slice_all[...].reshape(gram_all.shape[1:])

    def all_copy(step):
        return over_x(
            gram_all.at[grp], gram_all.at[grp], all_send.at[step], all_recv.at[step], group(step))

    def all_arrival(step):
        came = group(n_grp - step)
        return over_x(gram_all.at[came], gram_all.at[came], all_send.at[step], all_recv.at[step], came)

    for step in range(1, n_grp):
        all_copy(step).start()
    for step in range(1, n_grp):
        all_arrival(step).wait_recv()

    scale = math.sqrt(n_rows * RBD * LANES)
    order = work.shape[0]
    eliminate(gram_all[...].reshape(order, order), work)
    place_row = lax.broadcasted_iota(jnp.int32, (order, order), 0)
    place_col = lax.broadcasted_iota(jnp.int32, (order, order), 1)
    factor_ref[...] = jnp.where(place_col >= place_row, work[:, :order], 0.0) * (1.0 / scale)
    solved = jnp.dot(
        work[:, order:], y_value, precision=lax.Precision.HIGHEST, preferred_element_type=jnp.float32)
    basis_ref[...] = solved.T * scale

    def drain(step, carry):
        want_copy(step).wait_send()
        ghost_copy(step).wait_send()
        contrib_copy(step).wait_send()
        wg_copy(step).wait_send()
        return carry

    lax.fori_loop(1, n_rows, drain, 0)
    for step in range(1, n_grp):
        meta_copy(step).wait_send()
        omega_copy(step).wait_send()
        y_copy(step).wait_send()
        gram_copy(step).wait_send()
        all_copy(step).wait_send()
    for step in range(1, inner):
        part_copy(step).wait_send()
        back_copy(step).wait_send()
    for step in range(1, outer):
        row_copy(step).wait_send()
    for c in range(chunks):
        to_right(c).wait_send()
        to_left(c).wait_send()
        forward(c).wait_send()


BLOCK = 32


def eliminate(gram, work):
    order = gram.shape[0]
    work[:, :order] = gram
    place_row = lax.broadcasted_iota(jnp.int32, (order, order), 0)
    place_col = lax.broadcasted_iota(jnp.int32, (order, order), 1)
    work[:, order:] = jnp.where(place_row == place_col, 1.0, 0.0)
    small_row = lax.broadcasted_iota(jnp.int32, (BLOCK, BLOCK), 0)
    small_col = lax.broadcasted_iota(jnp.int32, (BLOCK, BLOCK), 1)
    for first in range(0, order, BLOCK):
        after = first + BLOCK
        low = first // LANES * LANES
        high = order + low + LANES
        left = work[first:after, first:after]
        right = jnp.where(small_row == small_col, 1.0, 0.0)
        for k in range(BLOCK):
            unit = lax.rsqrt(left[k:k + 1, k:k + 1])
            rows_left = left[k:k + 1, :] * unit
            rows_right = right[k:k + 1, :] * unit
            column = jnp.where(small_row[:, :1] > k, left[:, k:k + 1] * unit, 0.0)
            left = jnp.where(small_row == k, rows_left, left - column * rows_left)
            right = jnp.where(small_row == k, rows_right, right - column * rows_right)
        done = jnp.dot(
            right, work[first:after, low:high], precision=lax.Precision.HIGHEST, preferred_element_type=jnp.float32)
        work[first:after, low:high] = done
        if after < order:
            work[after:, low:high] = work[after:, low:high] - lax.dot_general(
                done[:, after - low:order - low], done, (((0,), (0,)), ((), ())),
                precision=lax.Precision.HIGHEST, preferred_element_type=jnp.float32)


def apply_all(tiles, omega_parts, meta, want_row, n_rows, n_grp, chunks):
    slots, tile, _ = tiles.shape
    owned = RBD // n_grp
    width = omega_parts.shape[2]
    block = (width, tile)
    order = width * n_grp
    inner = 8 if n_rows % 8 == 0 else n_rows
    some = width // inner
    bf16, f32, i32 = jnp.bfloat16, jnp.float32, jnp.int32
    dma = lambda count: pltpu.SemaphoreType.DMA((count,))
    vmem = pl.BlockSpec(memory_space=pltpu.VMEM)
    scratch = [
        pltpu.VMEM((n_grp, slots, tile, tile), bf16),
        pltpu.VMEM((n_grp, 8, LANES), i32),
        pltpu.SMEM((n_grp, 8, LANES), i32),
        pltpu.VMEM((n_rows, 1, LANES), i32),
        pltpu.SMEM((n_rows, 1, LANES), i32),
        pltpu.VMEM((n_rows, 1, LANES), i32),
        pltpu.SMEM((n_rows, 1, LANES), i32),
        pltpu.VMEM((RBD, LANES), i32),
        pltpu.SMEM((RBD, LANES), i32),
        pltpu.VMEM((RBD,) + block, bf16),
        pltpu.VMEM((n_rows,) + block, bf16),
        pltpu.VMEM((n_rows,) + block, bf16),
        pltpu.VMEM((n_grp, slots + 1) + block, f32),
        pltpu.VMEM((RBD,) + block, bf16),
        pltpu.VMEM((n_rows,) + block, bf16),
        pltpu.VMEM((n_rows,) + block, bf16),
        pltpu.VMEM((n_rows + 1,) + block, f32),
        pltpu.VMEM((RBD,) + block, bf16),
        pltpu.VMEM((n_rows,) + block, bf16),
        pltpu.VMEM((n_rows,) + block, bf16),
        pltpu.VMEM((RBD,) + block, f32),
        pltpu.VMEM((n_grp, owned) + block, f32),
        pltpu.VMEM((order, owned * tile), f32),
        pltpu.VMEM((n_grp, width, order), f32),
        pltpu.VMEM((n_grp, width, order), f32),
        pltpu.VMEM((inner, some, order), f32),
        pltpu.VMEM((inner, some, order), f32),
        pltpu.VMEM((some, order), f32),
        pltpu.VMEM((n_rows // inner, some, order), f32),
        pltpu.VMEM((inner, some, order), f32),
        pltpu.VMEM((n_grp, width, order), f32),
        pltpu.VMEM((order, 2 * order), f32),
        dma(3), dma(n_grp), dma(n_grp), dma(n_grp), dma(n_grp), dma(n_rows), dma(n_rows),
        dma(chunks), dma(chunks), dma(chunks), dma(chunks), dma(chunks), dma(chunks),
        dma(n_rows), dma(n_rows), dma(n_rows), dma(n_rows), dma(n_rows), dma(n_rows), dma(n_grp), dma(n_grp),
        dma(n_grp), dma(n_grp), dma(inner), dma(inner), dma(n_rows // inner), dma(n_rows // inner),
        dma(inner), dma(inner), dma(n_grp), dma(n_grp),
    ]
    return pl.pallas_call(
        functools.partial(apply_kernel, n_rows, n_grp, slots, chunks),
        out_shape=(
            jax.ShapeDtypeStruct((owned * tile, order), f32),
            jax.ShapeDtypeStruct((order, order), f32),
        ),
        in_specs=[pl.BlockSpec(memory_space=pl.ANY), vmem, vmem, vmem],
        out_specs=(vmem, vmem),
        scratch_shapes=scratch,
        compiler_params=pltpu.CompilerParams(
            collective_id=0, has_side_effects=True, vmem_limit_bytes=40 * 1024 * 1024),
        name="apply_all",
    )(tiles, omega_parts, meta, want_row)


def per_device(tiles, tile_row, tile_slot, tile_count, want, omega):
    tile = tiles.shape[-1]
    slots = tiles.shape[2]
    columns = omega.shape[1]
    n_rows = lax.axis_size("rows")
    n_grp = lax.axis_size("grp")
    chunks = 8 if slots % 8 == 0 and slots >= 48 else 2
    owned = RBD // n_grp
    meta = chains(tile_row.reshape(slots), tile_slot.reshape(slots), tile_count.reshape(()))
    want_row = jnp.pad(want.reshape(1, n_rows), ((0, 0), (0, LANES - n_rows)))
    omega_parts = omega.reshape(owned, tile, n_grp, columns // n_grp).transpose(2, 0, 3, 1)
    return apply_all(tiles.reshape(slots, tile, tile), omega_parts, meta, want_row, n_rows, n_grp, chunks)


def solution(mesh):
    return jax.shard_map(
        per_device,
        mesh=mesh,
        in_specs=(
            P("rows", "grp", None, None, None),
            P("rows", "grp", None),
            P("rows", "grp", None),
            P("rows", "grp"),
            P("rows", None),
            P(("rows", "grp"), None),
        ),
        out_specs=(P(("rows", "grp"), None), P()),
        check_vma=False,
    )
```

```python
import functools
import math

import jax
import jax.numpy as jnp
from jax import lax
from jax.experimental import pallas as pl
from jax.experimental.pallas import tpu as pltpu
from jax.sharding import PartitionSpec as P

RBD = 8
LANES = 128
MESH = pl.DeviceIdType.MESH
SLOT, ROW, PREV_ROW, PREV_SLOT, LAST_ROW, LAST_SLOT = range(6)


def chains(rows, slots, count, meta):
    shape = (LANES, LANES)
    earlier = lax.broadcasted_iota(jnp.int32, shape, 0)
    lane = lax.broadcasted_iota(jnp.int32, shape, 1)
    live = earlier < count
    lane_value = lane.astype(jnp.float32)
    for key, prev_key, last_key, values in ((ROW, PREV_ROW, LAST_ROW, rows), (SLOT, PREV_SLOT, LAST_SLOT, slots)):
        across = jnp.broadcast_to(values.astype(jnp.float32), shape)
        down = across.T
        meta[key:key + 1] = values
        hit = live & (earlier < lane) & (across == down)
        meta[prev_key:prev_key + 1] = jnp.max(jnp.where(hit, earlier + 1, 0), axis=0, keepdims=True)
        hit = live & (lane_value == down)
        meta[last_key:last_key + 1] = jnp.max(jnp.where(hit, earlier + 1, 0), axis=0, keepdims=True)


def apply_kernel(
    n_rows, n_grp, slots, chunks,
    tiles_ref, row_ref, slot_ref, count_ref, want_ref, omega_ref, basis_ref, factor_ref,
    row_v, slot_v, count_v, want_v, omega_v, keys, omega_parts,
    tbuf, meta_all, meta_s, want_all, want_s, prev_v, prev_s, last_v, last_s,
    omega_all, ghosts, ghost_out, partial, z_blocks,
    contrib_out, contrib_in, w_partial, w_blocks, w_ghosts, w_ghost_out, y_blocks, y_in,
    y_all, gram_out, gram_in, row_out, row_in, gram_all, work,
    in_sem, local_sem, small_send, small_recv, omega_send, omega_recv, want_send, want_recv,
    right_send, right_recv, left_send, left_recv, fwd_send, fwd_recv,
    ghost_send, ghost_recv, contrib_send, contrib_recv, wg_send, wg_recv, y_send, y_recv,
    gram_send, gram_recv, row_send, row_recv, all_send, all_recv,
):
    me = lax.axis_index("rows")
    grp = lax.axis_index("grp")
    per = slots // chunks
    owned = RBD // n_grp
    group = lambda step: lax.rem(grp + step, n_grp)
    peer = lambda step: lax.rem(me + step, n_rows)
    right, left = group(1), group(n_grp - 1)

    barrier = pltpu.get_barrier_semaphore()

    def greet(step, carry):
        pl.semaphore_signal(barrier, inc=1, device_id={"rows": peer(step)}, device_id_type=MESH)
        return carry

    for step in range(1, n_grp):
        pl.semaphore_signal(barrier, inc=1, device_id={"grp": group(step)}, device_id_type=MESH)
    lax.fori_loop(1, n_rows, greet, 0)
    inner = gram_out.shape[1]
    spot = lax.rem(me, inner)
    level = lax.div(me, inner)

    def near(far, step):
        return {"rows": level * inner + lax.rem(spot + step, inner), "grp": lax.rem(grp + far, n_grp)}

    def greet_near(step, carry):
        for far in range(1, n_grp):
            pl.semaphore_signal(barrier, inc=1, device_id=near(far, step), device_id_type=MESH)
        return carry

    lax.fori_loop(1, inner, greet_near, 0)

    brought = [
        pltpu.make_async_copy(src, dst, in_sem.at[i])
        for i, (src, dst) in enumerate(
            ((omega_ref, omega_v), (row_ref, row_v), (slot_ref, slot_v), (count_ref, count_v), (want_ref, want_v)))
    ]
    own_tiles = pltpu.make_async_copy(tiles_ref.at[0, 0], tbuf.at[0], local_sem.at[0])
    for copy in brought:
        copy.start()
    own_tiles.start()
    keys[...] = jnp.zeros(keys.shape, jnp.int32)
    partial[:, 0] = jnp.zeros((n_grp,) + partial.shape[2:], jnp.float32)
    w_partial[0] = jnp.zeros(w_partial.shape[1:], jnp.float32)
    for copy in brought:
        copy.wait()
    keys[0:1, :slots] = row_v[0]
    keys[1:2, :slots] = slot_v[0]
    keys[2:3, :n_rows] = want_v[...]
    meta_all[0] = jnp.zeros(meta_all.shape[1:], jnp.int32)
    chains(keys[0:1], keys[1:2], count_v[...], meta_all.at[0])
    want_all[me] = keys[2:3]
    width = omega_parts.shape[2]
    turned = omega_v[...].astype(jnp.float32).T.astype(jnp.bfloat16)
    for g in range(n_grp):
        for j in range(owned):
            omega_parts[g, j] = turned[g * width:(g + 1) * width, j * LANES:(j + 1) * LANES]
    for j in range(owned):
        omega_all[grp * owned + j] = omega_parts[grp, j]

    pl.semaphore_wait(barrier, n_rows - 1 + (n_grp - 1) * inner)

    def over_x(src, dst, send, recv, to):
        return pltpu.make_async_remote_copy(
            src_ref=src, dst_ref=dst, send_sem=send, recv_sem=recv, device_id={"grp": to}, device_id_type=MESH)

    def over_rows(src, dst, send, recv, to):
        return pltpu.make_async_remote_copy(
            src_ref=src, dst_ref=dst, send_sem=send, recv_sem=recv, device_id={"rows": to}, device_id_type=MESH)

    def want_copy(step):
        return over_rows(keys.at[pl.ds(2, 1)], want_all.at[me], want_send.at[step], want_recv.at[step], peer(step))

    def want_arrival(step):
        came = lax.rem(me - step + n_rows, n_rows)
        return over_rows(keys.at[pl.ds(2, 1)], want_all.at[came], want_send.at[step], want_recv.at[step], peer(step))

    def meta_copy(step):
        place = (0, 1, 3, 2)[step]
        return over_x(meta_all.at[0], meta_all.at[place], small_send.at[step], small_recv.at[step], group(step))

    def omega_copy(step):
        to = group(step)
        return over_x(
            omega_parts.at[to], omega_all.at[pl.ds(grp * owned, owned)], omega_send.at[step], omega_recv.at[step], to)

    def omega_arrival(step):
        came = group(n_grp - step)
        return over_x(
            omega_parts.at[came], omega_all.at[pl.ds(came * owned, owned)], omega_send.at[step], omega_recv.at[step], came)

    def start_want(step, carry):
        want_copy(step).start()
        return carry

    lax.fori_loop(1, n_rows, start_want, 0)
    for step in range(1, n_grp):
        omega_copy(step).start()
        meta_copy(step).start()

    def to_right(c):
        part = pl.ds(c * per, per)
        return over_x(tiles_ref.at[0, 0, part], tbuf.at[1, part], right_send.at[c], right_recv.at[c], right)

    def to_left(c):
        part = pl.ds(c * per, per)
        return over_x(tiles_ref.at[0, 0, part], tbuf.at[2, part], left_send.at[c], left_recv.at[c], left)

    def forward(c):
        part = pl.ds(c * per, per)
        if c < chunks // 2:
            return over_x(tbuf.at[1, part], tbuf.at[3, part], fwd_send.at[c], fwd_recv.at[c], right)
        return over_x(tbuf.at[2, part], tbuf.at[3, part], fwd_send.at[c], fwd_recv.at[c], left)

    for c in range(chunks):
        to_right(c).start()
        to_left(c).start()


    def wait_want(step, carry):
        want_arrival(step).wait_recv()
        return carry

    lax.fori_loop(1, n_rows, wait_want, 0)
    want_down = pltpu.make_async_copy(want_all, want_s, local_sem.at[1])
    want_down.start()
    for step in range(1, n_grp):
        meta_copy(step).wait_recv()
        omega_arrival(step).wait_recv()
    meta_down = pltpu.make_async_copy(meta_all, meta_s, local_sem.at[2])
    meta_down.start()
    want_down.wait()
    meta_down.wait()

    def ghost_copy(step):
        return over_rows(ghost_out.at[step], ghosts.at[step], ghost_send.at[step], ghost_recv.at[step], peer(step))

    def start_ghost(step, carry):
        ghost_out[step] = omega_all[want_s[peer(step), 0, me]]
        ghost_copy(step).start()
        return carry

    ghosts[0] = omega_all[want_s[me, 0, me]]
    lax.fori_loop(1, n_rows, start_ghost, 0)

    blocks = lax.broadcasted_iota(jnp.int32, (RBD, LANES), 0)

    def link(step, last):
        row = want_all[lax.rem(me - step + n_rows, n_rows)]
        hit = blocks == row
        prev_v[step] = jnp.max(jnp.where(hit, last, 0), axis=0, keepdims=True)
        return jnp.where(hit, step + 1, last)

    last_v[...] = lax.fori_loop(0, n_rows, link, jnp.zeros((RBD, LANES), jnp.int32))
    prev_down = pltpu.make_async_copy(prev_v, prev_s, local_sem.at[1])
    last_down = pltpu.make_async_copy(last_v, last_s, local_sem.at[2])
    prev_down.start()
    last_down.start()
    prev_down.wait()
    last_down.wait()

    own_tiles.wait()
    for c in range(chunks):
        to_right(c).wait_recv()
        if c < chunks // 2:
            forward(c).start()
        to_left(c).wait_recv()
        if c >= chunks // 2:
            forward(c).start()

    def wait_ghost(step, carry):
        ghost_copy(step).wait_recv()
        return carry

    lax.fori_loop(1, n_rows, wait_ghost, 0)

    unroll = per

    def multiply(place, first, source, by_row, sent):
        prev_key = PREV_ROW if by_row else PREV_SLOT
        products = []
        for i in range(unroll):
            t = first + i
            tile = tbuf[place, t]
            if by_row:
                slot = meta_s[place, SLOT, t]
                block = source[lax.rem(me - slot + n_rows, n_rows)]
                product = lax.dot_general(block, tile, (((1,), (1,)), ((), ())), preferred_element_type=jnp.float32)
            else:
                block = source[meta_s[place, ROW, t]]
                product = lax.dot_general(block, tile, (((1,), (0,)), ((), ())), preferred_element_type=jnp.float32)
            products.append(product)
        for i in range(unroll):
            t = first + i
            partial[place, t + 1] = products[i] + partial[place, meta_s[place, prev_key, t]]

    def whole(place, source, by_row):
        def step(c, carry):
            multiply(place, c * unroll, source, by_row, None)
            return carry
        lax.fori_loop(0, slots // unroll, step, 0)

    def total(key, index):
        value = partial[0, meta_s[0, key, index]]
        for place in range(1, n_grp):
            value = value + partial[place, meta_s[place, key, index]]
        return value

    for place in range(3):
        whole(place, ghosts, True)
    for c in range(chunks):
        forward(c).wait_recv()
        multiply(3, c * per, ghosts, True, None)

    def close_z(b, carry):
        z_blocks[b] = total(LAST_ROW, b).astype(jnp.bfloat16)
        return carry

    lax.fori_loop(0, RBD, close_z, 0)

    for place in range(n_grp):
        whole(place, z_blocks, False)

    def contrib_copy(step):
        return over_rows(
            contrib_out.at[step], contrib_in.at[step], contrib_send.at[step], contrib_recv.at[step], peer(step))

    contrib_in[0] = total(LAST_SLOT, me).astype(jnp.bfloat16)

    def start_contrib(step, carry):
        contrib_out[step] = total(LAST_SLOT, peer(step)).astype(jnp.bfloat16)
        contrib_copy(step).start()
        return carry

    lax.fori_loop(1, n_rows, start_contrib, 0)

    def add_contrib(step):
        w_partial[step + 1] = contrib_in[step].astype(jnp.float32) + w_partial[prev_s[step, 0, me]]

    add_contrib(0)

    def take_contrib(step, carry):
        contrib_copy(step).wait_recv()
        add_contrib(step)
        return carry

    lax.fori_loop(1, n_rows, take_contrib, 0)

    def close_w(b, carry):
        w_blocks[b] = w_partial[last_s[b, me]].astype(jnp.bfloat16)
        return carry

    lax.fori_loop(0, RBD, close_w, 0)

    def wg_copy(step):
        return over_rows(w_ghost_out.at[step], w_ghosts.at[step], wg_send.at[step], wg_recv.at[step], peer(step))

    def start_wg(step, carry):
        w_ghost_out[step] = w_blocks[want_s[peer(step), 0, me]]
        wg_copy(step).start()
        return carry

    def wait_wg(step, carry):
        wg_copy(step).wait_recv()
        return carry

    w_ghosts[0] = w_blocks[want_s[me, 0, me]]
    lax.fori_loop(1, n_rows, start_wg, 0)
    lax.fori_loop(1, n_rows, wait_wg, 0)

    for place in range(n_grp):
        whole(place, w_ghosts, True)

    def close_y(b, carry):
        y_blocks[b] = total(LAST_ROW, b)
        return carry

    lax.fori_loop(0, RBD, close_y, 0)

    def y_copy(step):
        to = group(step)
        return over_x(
            y_blocks.at[pl.ds(to * owned, owned)], y_in.at[step], y_send.at[step], y_recv.at[step], to)

    for step in range(1, n_grp):
        y_copy(step).start()
    for j in range(owned):
        y_in[0, j] = y_blocks[grp * owned + j]
    for step in range(1, n_grp):
        y_copy(step).wait_recv()
    for step in range(n_grp):
        came = group(n_grp - step)
        for j in range(owned):
            y_all[pl.ds(pl.multiple_of(came * width, width), width), pl.ds(j * LANES, LANES)] = y_in[step, j]

    outer = n_rows // inner
    y_value = y_all[...]
    own_gram = lax.dot_general(
        y_value, y_value, (((1,), (1,)), ((), ())), precision=lax.Precision.HIGHEST, preferred_element_type=jnp.float32)
    gram_out[...] = own_gram.reshape(gram_out.shape)

    def to_near(src, dst, send, recv, far, step):
        return pltpu.make_async_remote_copy(
            src_ref=src, dst_ref=dst, send_sem=send.at[far, step], recv_sem=recv.at[far, step],
            device_id=near(far, step), device_id_type=MESH)

    def gram_copy(far, step):
        return to_near(
            gram_out.at[group(far), lax.rem(spot + step, inner)], gram_in.at[grp, spot], gram_send, gram_recv, far, step)

    def gram_arrival(far, step):
        came = (group(n_grp - far), lax.rem(spot + inner - step, inner))
        return to_near(gram_out.at[came], gram_in.at[came], gram_send, gram_recv, far, step)

    def all_copy(far, step):
        return to_near(gram_all.at[grp, spot], gram_all.at[grp, spot], all_send, all_recv, far, step)

    def all_arrival(far, step):
        came = (group(n_grp - far), lax.rem(spot + inner - step, inner))
        return to_near(gram_all.at[came], gram_all.at[came], all_send, all_recv, far, step)

    def every_near(act):
        for far in (2, 1, 3, 0):
            def one(step, carry, far=far):
                act(far, step)
                return carry
            lax.fori_loop(1 if far == 0 else 0, inner, one, 0)

    every_near(lambda far, step: gram_copy(far, step).start())
    gram_in[grp, spot] = gram_out[grp, spot]
    every_near(lambda far, step: gram_arrival(far, step).wait_recv())
    row_out[...] = jnp.sum(gram_in[...], axis=(0, 1))

    def across(step):
        return lax.rem(level + step, outer)

    def row_copy(step):
        return over_rows(
            row_out, row_in.at[level], row_send.at[step], row_recv.at[step], across(step) * inner + spot)

    def row_arrival(step):
        came = across(outer - step)
        return over_rows(row_out, row_in.at[came], row_send.at[step], row_recv.at[step], came * inner + spot)

    for step in range(1, outer):
        row_copy(step).start()
    row_in[level] = row_out[...]
    for step in range(1, outer):
        row_arrival(step).wait_recv()
    gram_all[grp, spot] = jnp.sum(row_in[...], axis=0)
    every_near(lambda far, step: all_copy(far, step).start())
    every_near(lambda far, step: all_arrival(far, step).wait_recv())

    scale = math.sqrt(n_rows * RBD * LANES)
    order = work.shape[0]
    eliminate(gram_all[...].reshape(order, order), work)
    place_row = lax.broadcasted_iota(jnp.int32, (order, order), 0)
    place_col = lax.broadcasted_iota(jnp.int32, (order, order), 1)
    factor_ref[...] = jnp.where(place_col >= place_row, work[:, :order], 0.0) * (1.0 / scale)
    solved = jnp.dot(
        work[:, order:], y_value, precision=lax.Precision.HIGHEST, preferred_element_type=jnp.float32)
    basis_ref[...] = solved.T * scale

    def drain(step, carry):
        want_copy(step).wait_send()
        ghost_copy(step).wait_send()
        contrib_copy(step).wait_send()
        wg_copy(step).wait_send()
        return carry

    lax.fori_loop(1, n_rows, drain, 0)
    for step in range(1, n_grp):
        meta_copy(step).wait_send()
        omega_copy(step).wait_send()
        y_copy(step).wait_send()
    every_near(lambda far, step: gram_copy(far, step).wait_send())
    every_near(lambda far, step: all_copy(far, step).wait_send())
    for step in range(1, outer):
        row_copy(step).wait_send()
    for c in range(chunks):
        to_right(c).wait_send()
        to_left(c).wait_send()
        forward(c).wait_send()


BLOCK = 64
EIGHT = 8


def invert_factor(matrix):
    size = matrix.shape[0]
    groups = size // EIGHT
    place_row = lax.broadcasted_iota(jnp.int32, (size, size), 0)
    place_col = lax.broadcasted_iota(jnp.int32, (size, size), 1)
    both = jnp.concatenate([matrix, jnp.where(place_row == place_col, 1.0, 0.0)], axis=1)
    rows = [both[EIGHT * r:EIGHT * (r + 1)] for r in range(groups)]
    spread = lambda values: jnp.broadcast_to(values, (EIGHT, 2 * size))
    within = lax.broadcasted_iota(jnp.int32, (EIGHT, 2 * size), 0)
    pivots = []
    for s in range(groups):
        columns = [
            [spread(rows[r][:, EIGHT * s + j:EIGHT * s + j + 1]) for j in range(EIGHT)] for r in range(s, groups)]
        kept = jnp.ones((EIGHT, 2 * size), jnp.float32)
        for k in range(EIGHT):
            pivot = spread(columns[0][k][k:k + 1])
            kept = jnp.where(within == k, pivot, kept)
            inverse = 1.0 / pivot
            ratio = [column[k] * inverse for column in columns]
            ratio[0] = jnp.where(within > k, ratio[0], 0.0)
            for j in range(k + 1, EIGHT):
                entry = spread(columns[0][j][k:k + 1])
                for r in range(groups - s):
                    columns[r][j] = columns[r][j] - ratio[r] * entry
            entry = spread(rows[s][k:k + 1])
            for r in range(groups - s):
                rows[s + r] = rows[s + r] - ratio[r] * entry
        pivots.append(kept)
    scaled = jnp.concatenate([rows[r] * lax.rsqrt(pivots[r]) for r in range(groups)], axis=0)
    return scaled[:, size:]


def eliminate(gram, work):
    order = gram.shape[0]
    work[:, :order] = gram
    place_row = lax.broadcasted_iota(jnp.int32, (order, order), 0)
    place_col = lax.broadcasted_iota(jnp.int32, (order, order), 1)
    work[:, order:] = jnp.where(place_row == place_col, 1.0, 0.0)
    for first in range(0, order, BLOCK):
        after = first + BLOCK
        low = first // LANES * LANES
        high = order + low + LANES
        inverse = invert_factor(work[first:after, first:after])
        done = jnp.dot(
            inverse, work[first:after, low:high], precision=lax.Precision.HIGHEST, preferred_element_type=jnp.float32)
        work[first:after, low:high] = done
        if after < order:
            work[after:, low:high] = work[after:, low:high] - lax.dot_general(
                done[:, after - low:order - low], done, (((0,), (0,)), ((), ())),
                precision=lax.Precision.HIGHEST, preferred_element_type=jnp.float32)


def per_device(tiles, tile_row, tile_slot, tile_count, want, omega):
    slots, tile = tiles.shape[2], tiles.shape[-1]
    order = omega.shape[1]
    n_rows = lax.axis_size("rows")
    n_grp = lax.axis_size("grp")
    chunks = 8 if slots % 8 == 0 and slots >= 48 else 2
    owned = RBD // n_grp
    width = order // n_grp
    block = (width, tile)
    inner = 8 if n_rows % 8 == 0 else n_rows
    some = width // inner
    bf16, f32, i32 = jnp.bfloat16, jnp.float32, jnp.int32
    dma = lambda count: pltpu.SemaphoreType.DMA((count,))
    near = pltpu.SemaphoreType.DMA((n_grp, inner))
    vmem = pl.BlockSpec(memory_space=pltpu.VMEM)
    scratch = [
        pltpu.VMEM((1, 1, slots), i32),
        pltpu.VMEM((1, 1, slots), i32),
        pltpu.VMEM((1, 1), i32),
        pltpu.VMEM((1, n_rows), i32),
        pltpu.VMEM((order, order), bf16),
        pltpu.VMEM((8, LANES), i32),
        pltpu.VMEM((n_grp, owned) + block, bf16),
        pltpu.VMEM((n_grp, slots, tile, tile), bf16),
        pltpu.VMEM((n_grp, 8, LANES), i32),
        pltpu.SMEM((n_grp, 8, LANES), i32),
        pltpu.VMEM((n_rows, 1, LANES), i32),
        pltpu.SMEM((n_rows, 1, LANES), i32),
        pltpu.VMEM((n_rows, 1, LANES), i32),
        pltpu.SMEM((n_rows, 1, LANES), i32),
        pltpu.VMEM((RBD, LANES), i32),
        pltpu.SMEM((RBD, LANES), i32),
        pltpu.VMEM((RBD,) + block, bf16),
        pltpu.VMEM((n_rows,) + block, bf16),
        pltpu.VMEM((n_rows,) + block, bf16),
        pltpu.VMEM((n_grp, slots + 1) + block, f32),
        pltpu.VMEM((RBD,) + block, bf16),
        pltpu.VMEM((n_rows,) + block, bf16),
        pltpu.VMEM((n_rows,) + block, bf16),
        pltpu.VMEM((n_rows + 1,) + block, f32),
        pltpu.VMEM((RBD,) + block, bf16),
        pltpu.VMEM((n_rows,) + block, bf16),
        pltpu.VMEM((n_rows,) + block, bf16),
        pltpu.VMEM((RBD,) + block, f32),
        pltpu.VMEM((n_grp, owned) + block, f32),
        pltpu.VMEM((order, owned * tile), f32),
        pltpu.VMEM((n_grp, inner, some, order), f32),
        pltpu.VMEM((n_grp, inner, some, order), f32),
        pltpu.VMEM((some, order), f32),
        pltpu.VMEM((n_rows // inner, some, order), f32),
        pltpu.VMEM((n_grp, inner, some, order), f32),
        pltpu.VMEM((order, 2 * order), f32),
        dma(5), dma(3), dma(n_grp), dma(n_grp), dma(n_grp), dma(n_grp), dma(n_rows), dma(n_rows),
        dma(chunks), dma(chunks), dma(chunks), dma(chunks), dma(chunks), dma(chunks),
        dma(n_rows), dma(n_rows), dma(n_rows), dma(n_rows), dma(n_rows), dma(n_rows), dma(n_grp), dma(n_grp),
        near, near, dma(n_rows // inner), dma(n_rows // inner), near, near,
    ]
    return pl.pallas_call(
        functools.partial(apply_kernel, n_rows, n_grp, slots, chunks),
        out_shape=(
            jax.ShapeDtypeStruct((owned * tile, order), f32),
            jax.ShapeDtypeStruct((order, order), f32),
        ),
        in_specs=[pl.BlockSpec(memory_space=pl.ANY)] * 6,
        out_specs=(vmem, vmem),
        scratch_shapes=scratch,
        compiler_params=pltpu.CompilerParams(
            collective_id=0, has_side_effects=True, vmem_limit_bytes=40 * 1024 * 1024),
        name="apply_all",
    )(tiles, tile_row, tile_slot, tile_count, want, omega)


def solution(mesh):
    return jax.shard_map(
        per_device,
        mesh=mesh,
        in_specs=(
            P("rows", "grp", None, None, None),
            P("rows", "grp", None),
            P("rows", "grp", None),
            P("rows", "grp"),
            P("rows", None),
            P(("rows", "grp"), None),
        ),
        out_specs=(P(("rows", "grp"), None), P()),
        check_vma=False,
    )
```

```python
import functools
import math

import jax
import jax.numpy as jnp
from jax import lax
from jax.experimental import pallas as pl
from jax.experimental.pallas import tpu as pltpu
from jax.sharding import PartitionSpec as P

RBD = 8
MANY = 48
LANES = 128
MESH = pl.DeviceIdType.MESH
SLOT, ROW, PREV_ROW, PREV_SLOT, LAST_ROW, LAST_SLOT = range(6)


def chains(rows, slots, count, meta):
    shape = (LANES, LANES)
    earlier = lax.broadcasted_iota(jnp.int32, shape, 0)
    lane = lax.broadcasted_iota(jnp.int32, shape, 1)
    live = earlier < count
    lane_value = lane.astype(jnp.float32)
    for key, prev_key, last_key, values in ((ROW, PREV_ROW, LAST_ROW, rows), (SLOT, PREV_SLOT, LAST_SLOT, slots)):
        across = jnp.broadcast_to(values.astype(jnp.float32), shape)
        down = across.T
        meta[key:key + 1] = values
        hit = live & (earlier < lane) & (across == down)
        meta[prev_key:prev_key + 1] = jnp.max(jnp.where(hit, earlier + 1, 0), axis=0, keepdims=True)
        hit = live & (lane_value == down)
        meta[last_key:last_key + 1] = jnp.max(jnp.where(hit, earlier + 1, 0), axis=0, keepdims=True)


def apply_kernel(
    n_rows, n_grp, slots, chunks,
    tiles_ref, row_ref, slot_ref, count_ref, want_ref, omega_ref, basis_ref, factor_ref,
    row_v, slot_v, count_v, want_v, omega_v, keys, omega_parts,
    tbuf, meta_all, meta_s, want_all, want_s, prev_v, prev_s, last_v, last_s,
    omega_all, ghosts, ghost_out, partial, z_blocks,
    contrib_out, contrib_in, w_partial, w_blocks, w_ghosts_0, w_ghosts_1, w_ghost_out, y_blocks, y_in,
    y_all, gram_whole, gram_out, gram_in, row_out, row_in, gram_all, work,
    in_sem, local_sem, small_send, small_recv, omega_send, omega_recv, want_sem,
    right_send, right_recv, left_send, left_recv, fwd_send, fwd_recv,
    ghost_sem, contrib_sem, wg_sem, y_send, y_recv,
    gram_sem, row_send, row_recv, all_sem,
):
    me = lax.axis_index("rows")
    grp = lax.axis_index("grp")
    per = slots // chunks
    owned = RBD // n_grp
    group = lambda step: lax.rem(grp + step, n_grp)
    peer = lambda step: lax.rem(me + step, n_rows)
    right, left = group(1), group(n_grp - 1)

    barrier = pltpu.get_barrier_semaphore()

    def greet(step, carry):
        pl.semaphore_signal(barrier, inc=1, device_id={"rows": peer(step)}, device_id_type=MESH)
        return carry

    for step in range(1, n_grp):
        pl.semaphore_signal(barrier, inc=1, device_id={"grp": group(step)}, device_id_type=MESH)
    lax.fori_loop(1, n_rows, greet, 0)
    inner = gram_out.shape[0] // n_grp
    spot = lax.rem(me, inner)
    level = lax.div(me, inner)

    def near(far, step):
        return {"rows": level * inner + lax.rem(spot + step, inner), "grp": lax.rem(grp + far, n_grp)}

    def greet_near(step, carry):
        for far in range(1, n_grp):
            pl.semaphore_signal(barrier, inc=1, device_id=near(far, step), device_id_type=MESH)
        return carry

    lax.fori_loop(1, inner, greet_near, 0)

    brought = [
        pltpu.make_async_copy(src, dst, in_sem.at[i])
        for i, (src, dst) in enumerate(
            ((omega_ref, omega_v), (row_ref, row_v), (slot_ref, slot_v), (count_ref, count_v), (want_ref, want_v)))
    ]
    own_tiles = pltpu.make_async_copy(tiles_ref.at[0, 0], tbuf.at[0], local_sem.at[0])
    for copy in brought:
        copy.start()
    own_tiles.start()
    keys[...] = jnp.zeros(keys.shape, jnp.int32)
    partial[:, 0] = jnp.zeros((n_grp,) + partial.shape[2:], jnp.float32)
    w_partial[0] = jnp.zeros(w_partial.shape[1:], jnp.float32)
    for copy in brought:
        copy.wait()
    keys[0:1, :slots] = row_v[0]
    keys[1:2, :slots] = slot_v[0]
    keys[2:3, :n_rows] = want_v[...]
    meta_all[0] = jnp.zeros(meta_all.shape[1:], jnp.int32)
    chains(keys[0:1], keys[1:2], count_v[...], meta_all.at[0])
    want_all[0] = keys[2:3]
    width = omega_parts.shape[2]
    turned = omega_v[...].astype(jnp.float32).T.astype(jnp.bfloat16)
    for g in range(n_grp):
        for j in range(owned):
            omega_parts[g, j] = turned[g * width:(g + 1) * width, j * LANES:(j + 1) * LANES]
    for j in range(owned):
        omega_all[grp * owned + j] = omega_parts[grp, j]

    pl.semaphore_wait(barrier, n_rows - 1 + (n_grp - 1) * inner)

    def over_x(src, dst, send, recv, to):
        return pltpu.make_async_remote_copy(
            src_ref=src, dst_ref=dst, send_sem=send, recv_sem=recv, device_id={"grp": to}, device_id_type=MESH)

    def over_rows(src, dst, send, recv, to):
        return pltpu.make_async_remote_copy(
            src_ref=src, dst_ref=dst, send_sem=send, recv_sem=recv, device_id={"rows": to}, device_id_type=MESH)

    peers = n_rows - 1

    def to_peers(buffer_out, buffer_in, sems):
        def copy(step):
            return over_rows(buffer_out.at[step], buffer_in.at[step], sems.at[0], sems.at[1], peer(step))

        def arrived():
            whole = buffer_in.at[pl.ds(1, peers)]
            pltpu.make_async_copy(whole, whole, sems.at[1]).wait()

        def sent():
            whole = buffer_out.at[pl.ds(1, peers)]
            pltpu.make_async_copy(whole, whole, sems.at[0]).wait()

        return copy, arrived, sent

    def each_peer(act):
        few = 7
        def body(i, carry):
            act([1 + i * few + j for j in range(few)])
            return carry
        lax.fori_loop(0, peers // few, body, 0)

    def want_copy(step):
        return over_rows(keys.at[pl.ds(2, 1)], want_all.at[step], want_sem.at[0], want_sem.at[1], peer(step))

    def meta_copy(step):
        place = (0, 1, 3, 2)[step]
        return over_x(meta_all.at[0], meta_all.at[place], small_send.at[step], small_recv.at[step], group(step))

    def omega_copy(step):
        to = group(step)
        return over_x(
            omega_parts.at[to], omega_all.at[pl.ds(grp * owned, owned)], omega_send.at[step], omega_recv.at[step], to)

    def omega_arrival(step):
        came = group(n_grp - step)
        return over_x(
            omega_parts.at[came], omega_all.at[pl.ds(came * owned, owned)], omega_send.at[step], omega_recv.at[step], came)

    def start_want(steps):
        for step in steps:
            want_copy(step).start()

    each_peer(start_want)
    for step in range(1, n_grp):
        omega_copy(step).start()
        meta_copy(step).start()

    def to_right(c):
        part = pl.ds(c * per, per)
        return over_x(tiles_ref.at[0, 0, part], tbuf.at[1, part], right_send.at[c], right_recv.at[c], right)

    def to_left(c):
        part = pl.ds(c * per, per)
        return over_x(tiles_ref.at[0, 0, part], tbuf.at[2, part], left_send.at[c], left_recv.at[c], left)

    def forward(c):
        part = pl.ds(c * per, per)
        if c < chunks // 2:
            return over_x(tbuf.at[1, part], tbuf.at[3, part], fwd_send.at[c], fwd_recv.at[c], right)
        return over_x(tbuf.at[2, part], tbuf.at[3, part], fwd_send.at[c], fwd_recv.at[c], left)

    for c in range(chunks):
        to_right(c).start()
        to_left(c).start()


    want_part = want_all.at[pl.ds(1, peers)]
    pltpu.make_async_copy(want_part, want_part, want_sem.at[1]).wait()
    want_down = pltpu.make_async_copy(want_all, want_s, local_sem.at[1])
    want_down.start()
    for step in range(1, n_grp):
        meta_copy(step).wait_recv()
        omega_arrival(step).wait_recv()
    meta_down = pltpu.make_async_copy(meta_all, meta_s, local_sem.at[2])
    meta_down.start()
    want_down.wait()
    meta_down.wait()

    ghost_copy, ghosts_arrived, ghosts_sent = to_peers(ghost_out, ghosts, ghost_sem)

    def start_ghosts(steps):
        blocks = [omega_all[want_s[n_rows - step, 0, me]] for step in steps]
        for step, block in zip(steps, blocks):
            ghost_out[step] = block
        for step in steps:
            ghost_copy(step).start()

    ghosts[0] = omega_all[want_s[0, 0, me]]
    each_peer(start_ghosts)

    blocks = lax.broadcasted_iota(jnp.int32, (RBD, LANES), 0)

    def link(step, last):
        row = want_all[step]
        hit = blocks == row
        prev_v[step] = jnp.max(jnp.where(hit, last, 0), axis=0, keepdims=True)
        return jnp.where(hit, step + 1, last)

    last_v[...] = lax.fori_loop(0, n_rows, link, jnp.zeros((RBD, LANES), jnp.int32))
    prev_down = pltpu.make_async_copy(prev_v, prev_s, local_sem.at[1])
    last_down = pltpu.make_async_copy(last_v, last_s, local_sem.at[2])
    prev_down.start()
    last_down.start()
    prev_down.wait()
    last_down.wait()

    own_tiles.wait()
    for c in range(chunks):
        to_right(c).wait_recv()
        if c < chunks // 2:
            forward(c).start()
        to_left(c).wait_recv()
        if c >= chunks // 2:
            forward(c).start()

    ghosts_arrived()

    half = partial.shape[3]
    halves = range(partial.shape[2])
    w_ghosts = (w_ghosts_0, w_ghosts_1)

    def chunk_z(place, first, count):
        products = []
        for i in range(count):
            block = ghosts[lax.rem(me - meta_s[place, SLOT, first + i] + n_rows, n_rows)]
            products.append(lax.dot_general(
                block, tbuf[place, first + i], (((1,), (1,)), ((), ())), preferred_element_type=jnp.float32))
        for i in range(count):
            before = partial[place, meta_s[place, PREV_ROW, first + i]]
            partial[place, first + i + 1] = products[i].reshape(before.shape) + before

    def chunk_w(place, first, count, h):
        products = []
        for i in range(count):
            block = z_blocks[meta_s[place, ROW, first + i], h]
            products.append(jnp.dot(block, tbuf[place, first + i], preferred_element_type=jnp.float32))
        for i in range(count):
            partial[place, first + i + 1, h] = (
                products[i] + partial[place, meta_s[place, PREV_SLOT, first + i], h])

    def chunk_y(place, first, count, h):
        products = []
        for i in range(count):
            block = w_ghosts[h][lax.rem(me - meta_s[place, SLOT, first + i] + n_rows, n_rows)]
            products.append(lax.dot_general(
                block, tbuf[place, first + i], (((1,), (1,)), ((), ())), preferred_element_type=jnp.float32))
        for i in range(count):
            partial[place, first + i + 1, h] = (
                products[i] + partial[place, meta_s[place, PREV_ROW, first + i], h])

    many = MANY if slots % MANY == 0 else per

    def every_chunk(places, act):
        for place in places:
            def step(c, carry, place=place):
                act(place, c * many, many)
                return carry
            lax.fori_loop(0, slots // many, step, 0)

    every_chunk(range(3), chunk_z)
    for c in range(chunks):
        forward(c).wait_recv()
        chunk_z(3, c * per, per)
    for b in range(RBD):
        value = partial[0, meta_s[0, LAST_ROW, b]]
        for place in range(1, n_grp):
            value = value + partial[place, meta_s[place, LAST_ROW, b]]
        z_blocks[b] = value.astype(jnp.bfloat16)

    def total(key, index, h):
        value = partial[0, meta_s[0, key, index], h]
        for place in range(1, n_grp):
            value = value + partial[place, meta_s[place, key, index], h]
        return value

    contribs = [to_peers(contrib_out.at[h], contrib_in.at[h], contrib_sem.at[h]) for h in halves]
    w_trips = [to_peers(w_ghost_out.at[h], w_ghosts[h], wg_sem.at[h]) for h in halves]
    for h in halves:
        every_chunk(range(n_grp), lambda place, first, count: chunk_w(place, first, count, h))

        def start_contribs(steps):
            blocks = [total(LAST_SLOT, peer(step), h).astype(jnp.bfloat16) for step in steps]
            for step, block in zip(steps, blocks):
                contrib_out[h, step] = block
            for step in steps:
                contribs[h][0](step).start()

        contrib_in[h, 0] = total(LAST_SLOT, me, h).astype(jnp.bfloat16)
        each_peer(start_contribs)

    for h in halves:
        contribs[h][1]()

        def add_contribs(steps):
            for step in steps:
                w_partial[step + 1] = contrib_in[h, step].astype(jnp.float32) + w_partial[prev_s[step, 0, me]]

        add_contribs([0])
        each_peer(add_contribs)
        for b in range(RBD):
            w_blocks[b] = w_partial[last_s[b, me]].astype(jnp.bfloat16)

        def start_w(steps):
            blocks = [w_blocks[want_s[n_rows - step, 0, me]] for step in steps]
            for step, block in zip(steps, blocks):
                w_ghost_out[h, step] = block
            for step in steps:
                w_trips[h][0](step).start()

        w_ghosts[h][0] = w_blocks[want_s[0, 0, me]]
        each_peer(start_w)

    for h in halves:
        w_trips[h][1]()
        every_chunk(range(n_grp), lambda place, first, count: chunk_y(place, first, count, h))
        for b in range(RBD):
            y_blocks[b, pl.ds(h * half, half)] = total(LAST_ROW, b, h)

    def y_copy(step):
        to = group(step)
        return over_x(
            y_blocks.at[pl.ds(to * owned, owned)], y_in.at[step], y_send.at[step], y_recv.at[step], to)

    for step in range(1, n_grp):
        y_copy(step).start()
    for j in range(owned):
        y_in[0, j] = y_blocks[grp * owned + j]
    for step in range(1, n_grp):
        y_copy(step).wait_recv()
    for step in range(n_grp):
        came = group(n_grp - step)
        for j in range(owned):
            y_all[pl.ds(pl.multiple_of(came * width, width), width), pl.ds(j * LANES, LANES)] = y_in[step, j]

    outer = n_rows // inner
    y_value = y_all[...]
    own_gram = lax.dot_general(
        y_value, y_value, (((1,), (1,)), ((), ())), precision=lax.Precision.HIGHEST, preferred_element_type=jnp.float32)
    gram_whole[...] = own_gram.reshape(gram_whole.shape)

    others = n_grp * inner - 1

    def to_near(src, dst, sems, far, step):
        return pltpu.make_async_remote_copy(
            src_ref=src, dst_ref=dst, send_sem=sems.at[0], recv_sem=sems.at[1],
            device_id=near(far, step), device_id_type=MESH)

    def part(far, step):
        return group(far) * inner + lax.rem(spot + step, inner)

    def gram_copy(far, step):
        at = far * inner + step
        return to_near(gram_out.at[at], gram_in.at[at], gram_sem, far, step)

    def all_copy(far, step):
        return to_near(gram_all.at[0], gram_all.at[far * inner + step], all_sem, far, step)

    def wait_others(buffer, sem):
        whole = buffer.at[pl.ds(1, others)]
        pltpu.make_async_copy(whole, whole, sem).wait()

    def every_near(act):
        for far in (2, 1, 3, 0):
            for step in range(1 if far == 0 else 0, inner):
                act(far, step)

    gram_in[0] = gram_whole[part(0, 0)]
    parts = [(far, step) for far in range(n_grp) for step in range(inner)]
    for far, step in parts[1:]:
        gram_out[far * inner + step] = gram_whole[part(far, step)]
    every_near(lambda far, step: gram_copy(far, step).start())
    wait_others(gram_in, gram_sem.at[1])
    row_out[...] = jnp.sum(gram_in[...], axis=0)

    def across(step):
        return lax.rem(level + step, outer)

    def row_copy(step):
        return over_rows(
            row_out, row_in.at[level], row_send.at[step], row_recv.at[step], across(step) * inner + spot)

    def row_arrival(step):
        came = across(outer - step)
        return over_rows(row_out, row_in.at[came], row_send.at[step], row_recv.at[step], came * inner + spot)

    for step in range(1, outer):
        row_copy(step).start()
    row_in[level] = row_out[...]
    for step in range(1, outer):
        row_arrival(step).wait_recv()
    gram_all[0] = jnp.sum(row_in[...], axis=0)
    every_near(lambda far, step: all_copy(far, step).start())
    wait_others(gram_all, all_sem.at[1])
    for far, step in parts:
        came = group(n_grp - far) * inner + lax.rem(spot + inner - step, inner)
        gram_whole[came] = gram_all[far * inner + step]

    scale = math.sqrt(n_rows * RBD * LANES)
    order = work.shape[0]
    eliminate(gram_whole[...].reshape(order, order), work)
    place_row = lax.broadcasted_iota(jnp.int32, (order, order), 0)
    place_col = lax.broadcasted_iota(jnp.int32, (order, order), 1)
    factor_ref[...] = jnp.where(place_col >= place_row, work[:, :order], 0.0) * (1.0 / scale)
    solved = jnp.dot(
        work[:, order:], y_value, precision=lax.Precision.HIGHEST, preferred_element_type=jnp.float32)
    basis_ref[...] = solved.T * scale

    pltpu.make_async_copy(want_part, want_part, want_sem.at[0]).wait()
    ghosts_sent()
    for h in halves:
        contribs[h][2]()
        w_trips[h][2]()
    for step in range(1, n_grp):
        meta_copy(step).wait_send()
        omega_copy(step).wait_send()
        y_copy(step).wait_send()
    wait_others(gram_out, gram_sem.at[0])
    wait_others(gram_all, all_sem.at[0])
    for step in range(1, outer):
        row_copy(step).wait_send()
    for c in range(chunks):
        to_right(c).wait_send()
        to_left(c).wait_send()
        forward(c).wait_send()


BLOCK = 64
EIGHT = 8


def invert_factor(matrix):
    size = matrix.shape[0]
    groups = size // EIGHT
    place_row = lax.broadcasted_iota(jnp.int32, (size, size), 0)
    place_col = lax.broadcasted_iota(jnp.int32, (size, size), 1)
    both = jnp.concatenate([matrix, jnp.where(place_row == place_col, 1.0, 0.0)], axis=1)
    rows = [both[EIGHT * r:EIGHT * (r + 1)] for r in range(groups)]
    spread = lambda values: jnp.broadcast_to(values, (EIGHT, 2 * size))
    within = lax.broadcasted_iota(jnp.int32, (EIGHT, 2 * size), 0)
    pivots = []
    for s in range(groups):
        columns = [
            [spread(rows[r][:, EIGHT * s + j:EIGHT * s + j + 1]) for j in range(EIGHT)] for r in range(s, groups)]
        kept = jnp.ones((EIGHT, 2 * size), jnp.float32)
        for k in range(EIGHT):
            pivot = spread(columns[0][k][k:k + 1])
            kept = jnp.where(within == k, pivot, kept)
            inverse = 1.0 / pivot
            ratio = [column[k] * inverse for column in columns]
            ratio[0] = jnp.where(within > k, ratio[0], 0.0)
            for j in range(k + 1, EIGHT):
                entry = spread(columns[0][j][k:k + 1])
                for r in range(groups - s):
                    columns[r][j] = columns[r][j] - ratio[r] * entry
            entry = spread(rows[s][k:k + 1])
            for r in range(groups - s):
                rows[s + r] = rows[s + r] - ratio[r] * entry
        pivots.append(kept)
    scaled = jnp.concatenate([rows[r] * lax.rsqrt(pivots[r]) for r in range(groups)], axis=0)
    return scaled[:, size:]


def eliminate(gram, work):
    order = gram.shape[0]
    work[:, :order] = gram
    place_row = lax.broadcasted_iota(jnp.int32, (order, order), 0)
    place_col = lax.broadcasted_iota(jnp.int32, (order, order), 1)
    work[:, order:] = jnp.where(place_row == place_col, 1.0, 0.0)
    for first in range(0, order, BLOCK):
        after = first + BLOCK
        low = first // LANES * LANES
        high = order + low + LANES
        inverse = invert_factor(work[first:after, first:after])
        done = jnp.dot(
            inverse, work[first:after, low:high], precision=lax.Precision.HIGHEST, preferred_element_type=jnp.float32)
        work[first:after, low:high] = done
        if after < order:
            work[after:, low:high] = work[after:, low:high] - lax.dot_general(
                done[:, after - low:order - low], done, (((0,), (0,)), ((), ())),
                precision=lax.Precision.HIGHEST, preferred_element_type=jnp.float32)


def per_device(tiles, tile_row, tile_slot, tile_count, want, omega):
    slots, tile = tiles.shape[2], tiles.shape[-1]
    order = omega.shape[1]
    n_rows = lax.axis_size("rows")
    n_grp = lax.axis_size("grp")
    chunks = 8 if slots % 8 == 0 and slots >= 48 else 2
    owned = RBD // n_grp
    width = order // n_grp
    block = (width, tile)
    split = (2, width // 2, tile)
    inner = 8 if n_rows % 8 == 0 else n_rows
    some = width // inner
    bf16, f32, i32 = jnp.bfloat16, jnp.float32, jnp.int32
    dma = lambda count: pltpu.SemaphoreType.DMA((count,))
    both = pltpu.SemaphoreType.DMA((2, 2))
    vmem = pl.BlockSpec(memory_space=pltpu.VMEM)
    scratch = [
        pltpu.VMEM((1, 1, slots), i32),
        pltpu.VMEM((1, 1, slots), i32),
        pltpu.VMEM((1, 1), i32),
        pltpu.VMEM((1, n_rows), i32),
        pltpu.VMEM((order, order), bf16),
        pltpu.VMEM((8, LANES), i32),
        pltpu.VMEM((n_grp, owned) + block, bf16),
        pltpu.VMEM((n_grp, slots, tile, tile), bf16),
        pltpu.VMEM((n_grp, 8, LANES), i32),
        pltpu.SMEM((n_grp, 8, LANES), i32),
        pltpu.VMEM((n_rows, 1, LANES), i32),
        pltpu.SMEM((n_rows, 1, LANES), i32),
        pltpu.VMEM((n_rows, 1, LANES), i32),
        pltpu.SMEM((n_rows, 1, LANES), i32),
        pltpu.VMEM((RBD, LANES), i32),
        pltpu.SMEM((RBD, LANES), i32),
        pltpu.VMEM((RBD,) + block, bf16),
        pltpu.VMEM((n_rows,) + block, bf16),
        pltpu.VMEM((n_rows,) + block, bf16),
        pltpu.VMEM((n_grp, slots + 1) + split, f32),
        pltpu.VMEM((RBD,) + split, bf16),
        pltpu.VMEM((2, n_rows) + split[1:], bf16),
        pltpu.VMEM((2, n_rows) + split[1:], bf16),
        pltpu.VMEM((n_rows + 1,) + split[1:], f32),
        pltpu.VMEM((RBD,) + split[1:], bf16),
        pltpu.VMEM((n_rows,) + split[1:], bf16),
        pltpu.VMEM((n_rows,) + split[1:], bf16),
        pltpu.VMEM((2, n_rows) + split[1:], bf16),
        pltpu.VMEM((RBD,) + block, f32),
        pltpu.VMEM((n_grp, owned) + block, f32),
        pltpu.VMEM((order, owned * tile), f32),
        pltpu.VMEM((n_grp * inner, some, order), f32),
        pltpu.VMEM((n_grp * inner, some, order), f32),
        pltpu.VMEM((n_grp * inner, some, order), f32),
        pltpu.VMEM((some, order), f32),
        pltpu.VMEM((n_rows // inner, some, order), f32),
        pltpu.VMEM((n_grp * inner, some, order), f32),
        pltpu.VMEM((order, 2 * order), f32),
        dma(5), dma(3), dma(n_grp), dma(n_grp), dma(n_grp), dma(n_grp), dma(2),
        dma(chunks), dma(chunks), dma(chunks), dma(chunks), dma(chunks), dma(chunks),
        dma(2), both, both, dma(n_grp), dma(n_grp),
        dma(2), dma(n_rows // inner), dma(n_rows // inner), dma(2),
    ]
    return pl.pallas_call(
        functools.partial(apply_kernel, n_rows, n_grp, slots, chunks),
        out_shape=(
            jax.ShapeDtypeStruct((owned * tile, order), f32),
            jax.ShapeDtypeStruct((order, order), f32),
        ),
        in_specs=[pl.BlockSpec(memory_space=pl.ANY)] * 6,
        out_specs=(vmem, vmem),
        scratch_shapes=scratch,
        compiler_params=pltpu.CompilerParams(
            collective_id=0, has_side_effects=True, vmem_limit_bytes=60 * 1024 * 1024),
        name="apply_all",
    )(tiles, tile_row, tile_slot, tile_count, want, omega)


def solution(mesh):
    return jax.shard_map(
        per_device,
        mesh=mesh,
        in_specs=(
            P("rows", "grp", None, None, None),
            P("rows", "grp", None),
            P("rows", "grp", None),
            P("rows", "grp"),
            P("rows", None),
            P(("rows", "grp"), None),
        ),
        out_specs=(P(("rows", "grp"), None), P()),
        check_vma=False,
    )
```

```python
import functools
import math

import jax
import jax.numpy as jnp
from jax import lax
from jax.experimental import pallas as pl
from jax.experimental.pallas import tpu as pltpu
from jax.sharding import PartitionSpec as P

RBD = 8
MANY = 48
LANES = 128
MESH = pl.DeviceIdType.MESH
SLOT, ROW, PREV_ROW, PREV_SLOT, LAST_ROW, LAST_SLOT = range(6)


def chains(rows, slots, count, meta):
    shape = (LANES, LANES)
    earlier = lax.broadcasted_iota(jnp.int32, shape, 0)
    lane = lax.broadcasted_iota(jnp.int32, shape, 1)
    live = earlier < count
    lane_value = lane.astype(jnp.float32)
    for key, prev_key, last_key, values in ((ROW, PREV_ROW, LAST_ROW, rows), (SLOT, PREV_SLOT, LAST_SLOT, slots)):
        across = jnp.broadcast_to(values.astype(jnp.float32), shape)
        down = across.T
        meta[key:key + 1] = values
        hit = live & (earlier < lane) & (across == down)
        meta[prev_key:prev_key + 1] = jnp.max(jnp.where(hit, earlier + 1, 0), axis=0, keepdims=True)
        hit = live & (lane_value == down)
        meta[last_key:last_key + 1] = jnp.max(jnp.where(hit, earlier + 1, 0), axis=0, keepdims=True)


def apply_kernel(
    n_rows, n_grp, slots, chunks,
    tiles_ref, row_ref, slot_ref, count_ref, want_ref, omega_ref, basis_ref, factor_ref,
    row_v, slot_v, count_v, want_v, omega_v, keys, omega_parts,
    tbuf, meta_all, meta_s, want_all, want_s, prev_v, prev_s, last_v, last_s,
    omega_all, ghosts, ghost_out, partial, z_blocks,
    contrib_out, contrib_in, w_partial, w_blocks, w_ghosts_0, w_ghosts_1, w_ghost_out, y_blocks, y_in,
    y_all, gram_whole, gram_out, gram_in, row_out, row_in, gram_all, work,
    in_sem, local_sem, small_send, small_recv, omega_send, omega_recv, want_sem,
    right_send, right_recv, left_send, left_recv, fwd_send, fwd_recv,
    ghost_sem, contrib_sem, wg_sem, y_send, y_recv,
    gram_sem, row_send, row_recv, all_sem,
):
    me = lax.axis_index("rows")
    grp = lax.axis_index("grp")
    per = slots // chunks
    owned = RBD // n_grp
    group = lambda step: lax.rem(grp + step, n_grp)
    peer = lambda step: lax.rem(me + step, n_rows)
    right, left = group(1), group(n_grp - 1)

    barrier = pltpu.get_barrier_semaphore()

    def greet(step, carry):
        pl.semaphore_signal(barrier, inc=1, device_id={"rows": peer(step)}, device_id_type=MESH)
        return carry

    lax.fori_loop(1, n_rows, lambda i, carry: greet(lax.rem(i + n_rows // 4, n_rows - 1) + 1, carry), 0)
    for step in range(1, n_grp):
        pl.semaphore_signal(barrier, inc=1, device_id={"grp": group(step)}, device_id_type=MESH)
    inner = gram_out.shape[0] // n_grp
    spot = lax.rem(me, inner)
    level = lax.div(me, inner)

    def near(far, step):
        return {"rows": level * inner + lax.rem(spot + step, inner), "grp": lax.rem(grp + far, n_grp)}

    def greet_near(step, carry):
        for far in range(1, n_grp):
            pl.semaphore_signal(barrier, inc=1, device_id=near(far, step), device_id_type=MESH)
        return carry

    lax.fori_loop(1, inner, greet_near, 0)

    brought = [
        pltpu.make_async_copy(src, dst, in_sem.at[i])
        for i, (src, dst) in enumerate(
            ((omega_ref, omega_v), (row_ref, row_v), (slot_ref, slot_v), (count_ref, count_v), (want_ref, want_v)))
    ]
    own_tiles = pltpu.make_async_copy(tiles_ref.at[0, 0], tbuf.at[0], local_sem.at[0])
    for copy in brought:
        copy.start()
    own_tiles.start()
    keys[...] = jnp.zeros(keys.shape, jnp.int32)
    partial[:, 0] = jnp.zeros((n_grp,) + partial.shape[2:], jnp.float32)
    w_partial[0] = jnp.zeros(w_partial.shape[1:], jnp.float32)
    for copy in brought:
        copy.wait()
    keys[0:1, :slots] = row_v[0]
    keys[1:2, :slots] = slot_v[0]
    keys[2:3, :n_rows] = want_v[...]
    meta_all[0] = jnp.zeros(meta_all.shape[1:], jnp.int32)
    chains(keys[0:1], keys[1:2], count_v[...], meta_all.at[0])
    want_all[0] = keys[2:3]
    width = omega_parts.shape[2]
    turned = omega_v[...].astype(jnp.float32).T.astype(jnp.bfloat16)
    for g in range(n_grp):
        for j in range(owned):
            omega_parts[g, j] = turned[g * width:(g + 1) * width, j * LANES:(j + 1) * LANES]
    for j in range(owned):
        omega_all[grp * owned + j] = omega_parts[grp, j]

    pl.semaphore_wait(barrier, n_rows - 1 + (n_grp - 1) * inner)

    def over_x(src, dst, send, recv, to):
        return pltpu.make_async_remote_copy(
            src_ref=src, dst_ref=dst, send_sem=send, recv_sem=recv, device_id={"grp": to}, device_id_type=MESH)

    def over_rows(src, dst, send, recv, to):
        return pltpu.make_async_remote_copy(
            src_ref=src, dst_ref=dst, send_sem=send, recv_sem=recv, device_id={"rows": to}, device_id_type=MESH)

    peers = n_rows - 1

    def to_peers(buffer_out, buffer_in, sems):
        def copy(step):
            return over_rows(buffer_out.at[step], buffer_in.at[step], sems.at[0], sems.at[1], peer(step))

        def arrived():
            whole = buffer_in.at[pl.ds(1, peers)]
            pltpu.make_async_copy(whole, whole, sems.at[1]).wait()

        def sent():
            whole = buffer_out.at[pl.ds(1, peers)]
            pltpu.make_async_copy(whole, whole, sems.at[0]).wait()

        return copy, arrived, sent

    def each_peer(act):
        few = 7
        def body(i, carry):
            act([1 + i * few + j for j in range(few)])
            return carry
        lax.fori_loop(0, peers // few, body, 0)

    def want_copy(step):
        return over_rows(keys.at[pl.ds(2, 1)], want_all.at[step], want_sem.at[0], want_sem.at[1], peer(step))

    def meta_copy(step):
        place = (0, 1, 3, 2)[step]
        return over_x(meta_all.at[0], meta_all.at[place], small_send.at[step], small_recv.at[step], group(step))

    def omega_copy(step):
        to = group(step)
        return over_x(
            omega_parts.at[to], omega_all.at[pl.ds(grp * owned, owned)], omega_send.at[step], omega_recv.at[step], to)

    def omega_arrival(step):
        came = group(n_grp - step)
        return over_x(
            omega_parts.at[came], omega_all.at[pl.ds(came * owned, owned)], omega_send.at[step], omega_recv.at[step], came)

    def start_want(steps):
        for step in steps:
            want_copy(step).start()

    for step in range(1, n_grp):
        omega_copy(step).start()
        meta_copy(step).start()

    def to_right(c):
        part = pl.ds(c * per, per)
        return over_x(tiles_ref.at[0, 0, part], tbuf.at[1, part], right_send.at[c], right_recv.at[c], right)

    def to_left(c):
        part = pl.ds(c * per, per)
        return over_x(tiles_ref.at[0, 0, part], tbuf.at[2, part], left_send.at[c], left_recv.at[c], left)

    def forward(c):
        part = pl.ds(c * per, per)
        if c < chunks // 2:
            return over_x(tbuf.at[1, part], tbuf.at[3, part], fwd_send.at[c], fwd_recv.at[c], right)
        return over_x(tbuf.at[2, part], tbuf.at[3, part], fwd_send.at[c], fwd_recv.at[c], left)

    for c in range(chunks):
        to_right(c).start()
        to_left(c).start()
    each_peer(start_want)


    want_part = want_all.at[pl.ds(1, peers)]
    pltpu.make_async_copy(want_part, want_part, want_sem.at[1]).wait()
    want_down = pltpu.make_async_copy(want_all, want_s, local_sem.at[1])
    want_down.start()
    for step in range(1, n_grp):
        meta_copy(step).wait_recv()
        omega_arrival(step).wait_recv()
    meta_down = pltpu.make_async_copy(meta_all, meta_s, local_sem.at[2])
    meta_down.start()
    want_down.wait()
    meta_down.wait()

    ghost_copy, ghosts_arrived, ghosts_sent = to_peers(ghost_out, ghosts, ghost_sem)

    def start_ghosts(steps):
        blocks = [omega_all[want_s[n_rows - step, 0, me]] for step in steps]
        for step, block in zip(steps, blocks):
            ghost_out[step] = block
        for step in steps:
            ghost_copy(step).start()

    ghosts[0] = omega_all[want_s[0, 0, me]]
    each_peer(start_ghosts)

    blocks = lax.broadcasted_iota(jnp.int32, (RBD, LANES), 0)

    def link(step, last):
        row = want_all[step]
        hit = blocks == row
        prev_v[step] = jnp.max(jnp.where(hit, last, 0), axis=0, keepdims=True)
        return jnp.where(hit, step + 1, last)

    last_v[...] = lax.fori_loop(0, n_rows, link, jnp.zeros((RBD, LANES), jnp.int32))
    prev_down = pltpu.make_async_copy(prev_v, prev_s, local_sem.at[1])
    last_down = pltpu.make_async_copy(last_v, last_s, local_sem.at[2])
    prev_down.start()
    last_down.start()
    prev_down.wait()
    last_down.wait()

    own_tiles.wait()
    for c in range(chunks):
        to_right(c).wait_recv()
        if c < chunks // 2:
            forward(c).start()
        to_left(c).wait_recv()
        if c >= chunks // 2:
            forward(c).start()

    ghosts_arrived()

    half = partial.shape[3]
    halves = range(partial.shape[2])
    w_ghosts = (w_ghosts_0, w_ghosts_1)

    def chunk_z(place, first, count):
        products = []
        for i in range(count):
            block = ghosts[lax.rem(me - meta_s[place, SLOT, first + i] + n_rows, n_rows)]
            products.append(lax.dot_general(
                block, tbuf[place, first + i], (((1,), (1,)), ((), ())), preferred_element_type=jnp.float32))
        for i in range(count):
            before = partial[place, meta_s[place, PREV_ROW, first + i]]
            partial[place, first + i + 1] = products[i].reshape(before.shape) + before

    def chunk_w(place, first, count, h):
        products = []
        for i in range(count):
            block = z_blocks[meta_s[place, ROW, first + i], h]
            products.append(jnp.dot(block, tbuf[place, first + i], preferred_element_type=jnp.float32))
        for i in range(count):
            partial[place, first + i + 1, h] = (
                products[i] + partial[place, meta_s[place, PREV_SLOT, first + i], h])

    def chunk_y(place, first, count, h):
        products = []
        for i in range(count):
            block = w_ghosts[h][lax.rem(me - meta_s[place, SLOT, first + i] + n_rows, n_rows)]
            products.append(lax.dot_general(
                block, tbuf[place, first + i], (((1,), (1,)), ((), ())), preferred_element_type=jnp.float32))
        for i in range(count):
            partial[place, first + i + 1, h] = (
                products[i] + partial[place, meta_s[place, PREV_ROW, first + i], h])

    many = MANY if slots % MANY == 0 else per

    def every_chunk(places, act):
        for place in places:
            def step(c, carry, place=place):
                act(place, c * many, many)
                return carry
            lax.fori_loop(0, slots // many, step, 0)

    every_chunk(range(3), chunk_z)
    for c in range(chunks):
        forward(c).wait_recv()
        chunk_z(3, c * per, per)
    for b in range(RBD):
        value = partial[0, meta_s[0, LAST_ROW, b]]
        for place in range(1, n_grp):
            value = value + partial[place, meta_s[place, LAST_ROW, b]]
        z_blocks[b] = value.astype(jnp.bfloat16)

    def total(key, index, h):
        value = partial[0, meta_s[0, key, index], h]
        for place in range(1, n_grp):
            value = value + partial[place, meta_s[place, key, index], h]
        return value

    contribs = [to_peers(contrib_out.at[h], contrib_in.at[h], contrib_sem.at[h]) for h in halves]
    w_trips = [to_peers(w_ghost_out.at[h], w_ghosts[h], wg_sem.at[h]) for h in halves]
    for h in halves:
        every_chunk(range(n_grp), lambda place, first, count: chunk_w(place, first, count, h))

        def start_contribs(steps):
            blocks = [total(LAST_SLOT, peer(step), h).astype(jnp.bfloat16) for step in steps]
            for step, block in zip(steps, blocks):
                contrib_out[h, step] = block
            for step in steps:
                contribs[h][0](step).start()

        contrib_in[h, 0] = total(LAST_SLOT, me, h).astype(jnp.bfloat16)
        each_peer(start_contribs)

    for h in halves:
        contribs[h][1]()

        def add_contribs(steps):
            for step in steps:
                w_partial[step + 1] = contrib_in[h, step].astype(jnp.float32) + w_partial[prev_s[step, 0, me]]

        add_contribs([0])
        each_peer(add_contribs)
        for b in range(RBD):
            w_blocks[b] = w_partial[last_s[b, me]].astype(jnp.bfloat16)

        def start_w(steps):
            blocks = [w_blocks[want_s[n_rows - step, 0, me]] for step in steps]
            for step, block in zip(steps, blocks):
                w_ghost_out[h, step] = block
            for step in steps:
                w_trips[h][0](step).start()

        w_ghosts[h][0] = w_blocks[want_s[0, 0, me]]
        each_peer(start_w)

    def y_copy(step, h):
        to = group(step)
        return over_x(
            y_blocks.at[h, pl.ds(to * owned, owned)], y_in.at[h, step], y_send.at[h, step], y_recv.at[h, step], to)

    for h in halves:
        w_trips[h][1]()
        every_chunk(range(n_grp), lambda place, first, count: chunk_y(place, first, count, h))
        for b in range(RBD):
            y_blocks[h, b] = total(LAST_ROW, b, h)
        for step in range(1, n_grp):
            y_copy(step, h).start()
    for h in halves:
        for step in range(1, n_grp):
            y_copy(step, h).wait_recv()
        for step in range(n_grp):
            came = group(n_grp - step)
            for j in range(owned):
                value = y_in[h, step, j] if step else y_blocks[h, grp * owned + j]
                y_all[pl.ds(pl.multiple_of(came * width + h * half, half), half), pl.ds(j * LANES, LANES)] = value

    outer = n_rows // inner
    y_value = y_all[...]
    own_gram = lax.dot_general(
        y_value, y_value, (((1,), (1,)), ((), ())), precision=lax.Precision.HIGHEST, preferred_element_type=jnp.float32)
    gram_whole[...] = own_gram.reshape(gram_whole.shape)

    others = n_grp * inner - 1

    def to_near(src, dst, sems, far, step):
        return pltpu.make_async_remote_copy(
            src_ref=src, dst_ref=dst, send_sem=sems.at[0], recv_sem=sems.at[1],
            device_id=near(far, step), device_id_type=MESH)

    def part(far, step):
        return group(far) * inner + lax.rem(spot + step, inner)

    def gram_copy(far, step):
        at = far * inner + step
        return to_near(gram_out.at[at], gram_in.at[at], gram_sem, far, step)

    def all_copy(far, step):
        return to_near(gram_all.at[0], gram_all.at[far * inner + step], all_sem, far, step)

    def wait_others(buffer, sem):
        whole = buffer.at[pl.ds(1, others)]
        pltpu.make_async_copy(whole, whole, sem).wait()

    def every_near(act):
        for far in (2, 1, 3, 0):
            for step in range(1 if far == 0 else 0, inner):
                act(far, step)

    gram_in[0] = gram_whole[part(0, 0)]
    parts = [(far, step) for far in range(n_grp) for step in range(inner)]
    for far, step in parts[1:]:
        gram_out[far * inner + step] = gram_whole[part(far, step)]
    every_near(lambda far, step: gram_copy(far, step).start())
    wait_others(gram_in, gram_sem.at[1])
    row_out[...] = jnp.sum(gram_in[...], axis=0)

    def across(step):
        return lax.rem(level + step, outer)

    def row_copy(step):
        return over_rows(
            row_out, row_in.at[level], row_send.at[step], row_recv.at[step], across(step) * inner + spot)

    def row_arrival(step):
        came = across(outer - step)
        return over_rows(row_out, row_in.at[came], row_send.at[step], row_recv.at[step], came * inner + spot)

    for step in range(1, outer):
        row_copy(step).start()
    row_in[level] = row_out[...]
    for step in range(1, outer):
        row_arrival(step).wait_recv()
    gram_all[0] = jnp.sum(row_in[...], axis=0)
    every_near(lambda far, step: all_copy(far, step).start())
    wait_others(gram_all, all_sem.at[1])
    for far, step in parts:
        came = group(n_grp - far) * inner + lax.rem(spot + inner - step, inner)
        gram_whole[came] = gram_all[far * inner + step]

    scale = math.sqrt(n_rows * RBD * LANES)
    order = work.shape[0]
    eliminate(gram_whole[...].reshape(order, order), work)
    place_row = lax.broadcasted_iota(jnp.int32, (order, order), 0)
    place_col = lax.broadcasted_iota(jnp.int32, (order, order), 1)
    factor_ref[...] = jnp.where(place_col >= place_row, work[:, :order], 0.0) * (1.0 / scale)
    solved = jnp.dot(
        work[:, order:], y_value, precision=lax.Precision.HIGHEST, preferred_element_type=jnp.float32)
    basis_ref[...] = solved.T * scale

    pltpu.make_async_copy(want_part, want_part, want_sem.at[0]).wait()
    ghosts_sent()
    for h in halves:
        contribs[h][2]()
        w_trips[h][2]()
    for step in range(1, n_grp):
        meta_copy(step).wait_send()
        omega_copy(step).wait_send()
        for h in halves:
            y_copy(step, h).wait_send()
    wait_others(gram_out, gram_sem.at[0])
    wait_others(gram_all, all_sem.at[0])
    for step in range(1, outer):
        row_copy(step).wait_send()
    for c in range(chunks):
        to_right(c).wait_send()
        to_left(c).wait_send()
        forward(c).wait_send()


BLOCK = 64
EIGHT = 8


def invert_factor(matrix):
    size = matrix.shape[0]
    groups = size // EIGHT
    place_row = lax.broadcasted_iota(jnp.int32, (size, size), 0)
    place_col = lax.broadcasted_iota(jnp.int32, (size, size), 1)
    both = jnp.concatenate([matrix, jnp.where(place_row == place_col, 1.0, 0.0)], axis=1)
    rows = [both[EIGHT * r:EIGHT * (r + 1)] for r in range(groups)]
    spread = lambda values: jnp.broadcast_to(values, (EIGHT, 2 * size))
    within = lax.broadcasted_iota(jnp.int32, (EIGHT, 2 * size), 0)
    pivots = []
    for s in range(groups):
        columns = [
            [spread(rows[r][:, EIGHT * s + j:EIGHT * s + j + 1]) for j in range(EIGHT)] for r in range(s, groups)]
        kept = jnp.ones((EIGHT, 2 * size), jnp.float32)
        for k in range(EIGHT):
            pivot = spread(columns[0][k][k:k + 1])
            kept = jnp.where(within == k, pivot, kept)
            inverse = 1.0 / pivot
            below = [column[k] for column in columns]
            below[0] = jnp.where(within > k, below[0], 0.0)
            for j in range(k + 1, EIGHT):
                entry = spread(columns[0][j][k:k + 1])
                for r in range(groups - s):
                    columns[r][j] = columns[r][j] - (below[r] * entry) * inverse
            entry = spread(rows[s][k:k + 1])
            for r in range(groups - s):
                rows[s + r] = rows[s + r] - (below[r] * entry) * inverse
        pivots.append(kept)
    scaled = jnp.concatenate([rows[r] * lax.rsqrt(pivots[r]) for r in range(groups)], axis=0)
    return scaled[:, size:]


def eliminate(gram, work):
    order = gram.shape[0]
    work[:, :order] = gram
    place_row = lax.broadcasted_iota(jnp.int32, (order, order), 0)
    place_col = lax.broadcasted_iota(jnp.int32, (order, order), 1)
    work[:, order:] = jnp.where(place_row == place_col, 1.0, 0.0)
    for first in range(0, order, BLOCK):
        after = first + BLOCK
        low = first // LANES * LANES
        high = order + low + LANES
        inverse = invert_factor(work[first:after, first:after])
        done = jnp.dot(
            inverse, work[first:after, low:high], precision=lax.Precision.HIGHEST, preferred_element_type=jnp.float32)
        work[first:after, low:high] = done
        if after < order:
            work[after:, low:high] = work[after:, low:high] - lax.dot_general(
                done[:, after - low:order - low], done, (((0,), (0,)), ((), ())),
                precision=lax.Precision.HIGHEST, preferred_element_type=jnp.float32)


def per_device(tiles, tile_row, tile_slot, tile_count, want, omega):
    slots, tile = tiles.shape[2], tiles.shape[-1]
    order = omega.shape[1]
    n_rows = lax.axis_size("rows")
    n_grp = lax.axis_size("grp")
    chunks = 8 if slots % 8 == 0 and slots >= 48 else 2
    owned = RBD // n_grp
    width = order // n_grp
    block = (width, tile)
    split = (2, width // 2, tile)
    inner = 8 if n_rows % 8 == 0 else n_rows
    some = width // inner
    bf16, f32, i32 = jnp.bfloat16, jnp.float32, jnp.int32
    dma = lambda count: pltpu.SemaphoreType.DMA((count,))
    both = pltpu.SemaphoreType.DMA((2, 2))
    vmem = pl.BlockSpec(memory_space=pltpu.VMEM)
    scratch = [
        pltpu.VMEM((1, 1, slots), i32),
        pltpu.VMEM((1, 1, slots), i32),
        pltpu.VMEM((1, 1), i32),
        pltpu.VMEM((1, n_rows), i32),
        pltpu.VMEM((order, order), bf16),
        pltpu.VMEM((8, LANES), i32),
        pltpu.VMEM((n_grp, owned) + block, bf16),
        pltpu.VMEM((n_grp, slots, tile, tile), bf16),
        pltpu.VMEM((n_grp, 8, LANES), i32),
        pltpu.SMEM((n_grp, 8, LANES), i32),
        pltpu.VMEM((n_rows, 1, LANES), i32),
        pltpu.SMEM((n_rows, 1, LANES), i32),
        pltpu.VMEM((n_rows, 1, LANES), i32),
        pltpu.SMEM((n_rows, 1, LANES), i32),
        pltpu.VMEM((RBD, LANES), i32),
        pltpu.SMEM((RBD, LANES), i32),
        pltpu.VMEM((RBD,) + block, bf16),
        pltpu.VMEM((n_rows,) + block, bf16),
        pltpu.VMEM((n_rows,) + block, bf16),
        pltpu.VMEM((n_grp, slots + 1) + split, f32),
        pltpu.VMEM((RBD,) + split, bf16),
        pltpu.VMEM((2, n_rows) + split[1:], bf16),
        pltpu.VMEM((2, n_rows) + split[1:], bf16),
        pltpu.VMEM((n_rows + 1,) + split[1:], f32),
        pltpu.VMEM((RBD,) + split[1:], bf16),
        pltpu.VMEM((n_rows,) + split[1:], bf16),
        pltpu.VMEM((n_rows,) + split[1:], bf16),
        pltpu.VMEM((2, n_rows) + split[1:], bf16),
        pltpu.VMEM((2, RBD) + split[1:], f32),
        pltpu.VMEM((2, n_grp, owned) + split[1:], f32),
        pltpu.VMEM((order, owned * tile), f32),
        pltpu.VMEM((n_grp * inner, some, order), f32),
        pltpu.VMEM((n_grp * inner, some, order), f32),
        pltpu.VMEM((n_grp * inner, some, order), f32),
        pltpu.VMEM((some, order), f32),
        pltpu.VMEM((n_rows // inner, some, order), f32),
        pltpu.VMEM((n_grp * inner, some, order), f32),
        pltpu.VMEM((order, 2 * order), f32),
        dma(5), dma(3), dma(n_grp), dma(n_grp), dma(n_grp), dma(n_grp), dma(2),
        dma(chunks), dma(chunks), dma(chunks), dma(chunks), dma(chunks), dma(chunks),
        dma(2), both, both, pltpu.SemaphoreType.DMA((2, n_grp)), pltpu.SemaphoreType.DMA((2, n_grp)),
        dma(2), dma(n_rows // inner), dma(n_rows // inner), dma(2),
    ]
    return pl.pallas_call(
        functools.partial(apply_kernel, n_rows, n_grp, slots, chunks),
        out_shape=(
            jax.ShapeDtypeStruct((owned * tile, order), f32),
            jax.ShapeDtypeStruct((order, order), f32),
        ),
        in_specs=[pl.BlockSpec(memory_space=pl.ANY)] * 6,
        out_specs=(vmem, vmem),
        scratch_shapes=scratch,
        compiler_params=pltpu.CompilerParams(
            collective_id=0, has_side_effects=True, vmem_limit_bytes=60 * 1024 * 1024),
        name="apply_all",
    )(tiles, tile_row, tile_slot, tile_count, want, omega)


def solution(mesh):
    return jax.shard_map(
        per_device,
        mesh=mesh,
        in_specs=(
            P("rows", "grp", None, None, None),
            P("rows", "grp", None),
            P("rows", "grp", None),
            P("rows", "grp"),
            P("rows", None),
            P(("rows", "grp"), None),
        ),
        out_specs=(P(("rows", "grp"), None), P()),
        check_vma=False,
    )
```
